256 devices in a mesh: flow: 32 (over x, y, core), cross: 8 (over z).
Axes of the slice: x: 4, y: 4, z: 8, core: 2. Of those that a mesh axis runs over, the one named last changes fastest.
Arguments:
- right_side: float32 [32, 16, 2, 8, 135], P('flow', 'cross'), may hold values from -6 to 6
- start_iterate: float32 [32, 16, 2, 8, 135], P('flow', 'cross'), may hold values from -6 to 6
- inverse_blocks: float32 [32, 16, 2, 135, 135], P('flow', 'cross'), may hold values from -2 to 2
- face_blocks: float32 [32, 6, 16, 2, 135, 135], P('flow', None, 'cross'), may hold values from -2 to 2
- color_order: int32 [32, 16, 2], P('flow', 'cross'), may hold values from 0 to 1, as said below
Outputs:
- sweep: float32 [32, 16, 2, 8, 135], P('flow', 'cross')
The draws below stay inside these ranges and needn't reach their ends.
Inputs may be any that keep to these rules, and one draw needn't show every extreme that they name: `color_order`: in every flow layer the colors form a checkerboard over cross columns and span positions: neighbours inside one layer have different colors.
All inputs are finite; a program needn't handle non-finite values.
Results may differ from the reference program's by a relative error of at most 0.0003.
Values sent between devices are 32-bit elements; how exact they have to be, the bound alone decides.
A program may use at most 128 MiB of HBM per device.

```python
import math
import jax
import jax.numpy as jnp
from jax import lax

B = 135
VECS = 8
C_DEV = 2
SPAN_ELEMENTS = 2
FLOW_LAYERS = 32
CROSS_COLUMNS = 16


def layer_rates(key):
    random_keys = jax.random.split(key, 5)
    diagonal = jax.random.uniform(random_keys[0], (FLOW_LAYERS, CROSS_COLUMNS, SPAN_ELEMENTS, B), jnp.float32, 0.7, 1.3)
    gradual_mode = jax.random.uniform(random_keys[1], (1, CROSS_COLUMNS, SPAN_ELEMENTS, B), jnp.float32) < 0.5
    retain_flag = jnp.exp(-jax.random.uniform(random_keys[2], (1, CROSS_COLUMNS, SPAN_ELEMENTS, B), jnp.float32, 0.5, 2.0) / FLOW_LAYERS)
    quick_mode = jax.random.uniform(random_keys[3], (FLOW_LAYERS, CROSS_COLUMNS, SPAN_ELEMENTS, B), jnp.float32, 0.4, 0.8)
    sudden_surge = jax.random.uniform(random_keys[4], (FLOW_LAYERS, CROSS_COLUMNS, SPAN_ELEMENTS, 1), jnp.float32) < 3.0 / FLOW_LAYERS
    remain_resident = jnp.where(gradual_mode, retain_flag, quick_mode) * jnp.where(sudden_surge, 0.6, 1.0)
    return (diagonal, remain_resident)


def draw_inverse_blocks(key, part):
    diagonal, remain_resident = layer_rates(key)
    key = jax.random.fold_in(key, 11)
    shape = (FLOW_LAYERS, CROSS_COLUMNS, SPAN_ELEMENTS, B, B)
    noise = jax.random.normal(key, shape, jnp.float32)
    eye = jnp.eye(B, dtype=jnp.float32)
    return noise * (0.3 / math.sqrt(B)) + diagonal[..., None] * eye


def draw_face_blocks(key, part):
    diagonal, remain_resident = layer_rates(key)
    key = jax.random.fold_in(key, 23)
    shape = (FLOW_LAYERS, 6, CROSS_COLUMNS, SPAN_ELEMENTS, B, B)
    noise = jax.random.normal(key, shape, jnp.float32)
    scales = jnp.array([0.2, 0.3, 0.25, 0.25, 0.25, 0.25], jnp.float32)[None, :, None, None, None, None] / math.sqrt(B)
    upward = (-remain_resident / diagonal)[:, None, :, :, :, None] * jnp.eye(B, dtype=jnp.float32)
    first_face = (jnp.arange(6) == 0).astype(jnp.float32)[None, :, None, None, None, None]
    return noise * scales + first_face * upward


def draw_color_order(key, part):
    key = jax.random.fold_in(key, 37)
    phase = jax.random.randint(key, (FLOW_LAYERS,), 0, 2, jnp.int32)
    columns = jnp.arange(CROSS_COLUMNS, dtype=jnp.int32)
    spans = jnp.arange(SPAN_ELEMENTS, dtype=jnp.int32)
    return ((columns[None, :, None] + spans[None, None, :] + phase[:, None, None]) % 2).astype(jnp.int32)


def steps_of(stream_key, shape, shards, smallest, top_value):
    def one(axis_at, parts):
        steps = jax.random.uniform(jax.random.fold_in(jax.random.fold_in(stream_key, 6), axis_at), (parts,), jnp.float32, smallest / len(shards), top_value / len(shards))
        return jnp.repeat(jnp.exp(steps), shape[axis_at] // parts).reshape((-1,) + (1,) * (len(shape) - axis_at - 1))

    factor_of = one(*shards[0])
    for cut in shards[1:]:
        factor_of = factor_of * one(*cut)
    return factor_of


def centred(rng, extent, width, bound, shards=(), held_as=jnp.bfloat16):
    result = jax.random.normal(rng, extent, jnp.float32) * width
    if len(shards) > 0:
        result = steps_of(rng, extent, shards, -0.22, 0.18) * result
    return jnp.clip(result, min=-bound, max=bound).astype(held_as)


def setup_inputs(seed: int = 0) -> dict:
    keys = jax.random.split(jax.random.key(seed), 6)
    right_side = centred(keys[0], (FLOW_LAYERS, CROSS_COLUMNS, SPAN_ELEMENTS, VECS, B), 1.0, 6.0, ((0, 32), (1, 8)), jnp.float32)
    start_iterate = centred(keys[1], (FLOW_LAYERS, CROSS_COLUMNS, SPAN_ELEMENTS, VECS, B), 1.0, 6.0, ((0, 32), (1, 8)), jnp.float32)
    inverse_blocks = draw_inverse_blocks(jax.random.fold_in(keys[5], 71), 0)
    face_blocks = draw_face_blocks(jax.random.fold_in(keys[5], 71), 0)
    color_order = draw_color_order(jax.random.fold_in(keys[5], 71), 0)
    return {"right_side": right_side, "start_iterate": start_iterate, "inverse_blocks": inverse_blocks, "face_blocks": face_blocks, "color_order": color_order}


def apply_blocks(blocks, vectors):
    return jnp.einsum("jkrc,jkvc->jkvr", blocks, vectors, precision=lax.Precision.HIGHEST)


def from_left(values):
    return jnp.pad(values[:-1], ((1, 0), (0, 0), (0, 0), (0, 0)))


def from_right(values):
    return jnp.pad(values[1:], ((0, 1), (0, 0), (0, 0), (0, 0)))


def from_back(values):
    return jnp.pad(values[:, :-1], ((0, 0), (1, 0), (0, 0), (0, 0)))


def from_front(values):
    return jnp.pad(values[:, 1:], ((0, 0), (0, 1), (0, 0), (0, 0)))


def sweep_layers(source_all, padded_old, next_old, inbound, inverse_blocks, face_blocks, color_order, keep_left, keep_right):
    def layer(upper, items):
        source, around, below, inverse, faces, colors = items
        old = around[1:-1]
        total = source - apply_blocks(faces[0], upper) - apply_blocks(faces[1], below)
        total = total - apply_blocks(faces[2], around[:-2]) - apply_blocks(faces[3], around[2:])
        total = total - apply_blocks(faces[4], from_back(old)) - apply_blocks(faces[5], from_front(old))
        first = apply_blocks(inverse, total)
        first_color = (colors == 0)[:, :, None, None]
        delta = jnp.where(first_color, first - old, jnp.zeros_like(first))
        correction = apply_blocks(faces[2], keep_left * from_left(delta)) + apply_blocks(faces[3], keep_right * from_right(delta))
        correction = correction + apply_blocks(faces[4], from_back(delta)) + apply_blocks(faces[5], from_front(delta))
        fresh = jnp.where(first_color, first, first - apply_blocks(inverse, correction))
        return fresh, fresh

    items = (source_all, padded_old, next_old, inverse_blocks, face_blocks, color_order)
    return lax.scan(layer, inbound, items)[1]


def reference(right_side, start_iterate, inverse_blocks, face_blocks, color_order):
    columns = jnp.arange(right_side.shape[1]) % C_DEV
    keep_left = (columns != 0).astype(right_side.dtype)[:, None, None, None]
    keep_right = (columns != C_DEV - 1).astype(right_side.dtype)[:, None, None, None]
    padded_old = jnp.pad(start_iterate, ((0, 0), (1, 1), (0, 0), (0, 0), (0, 0)))
    next_old = jnp.concatenate([start_iterate[1:], jnp.zeros_like(start_iterate[:1])], axis=0)
    inbound = jnp.zeros_like(right_side[0])
    return sweep_layers(right_side, padded_old, next_old, inbound, inverse_blocks, face_blocks, color_order, keep_left, keep_right)
```

```python
import functools

import jax
import jax.numpy as jnp
from jax import lax
from jax.experimental import pallas as pl
from jax.experimental.pallas import tpu as pltpu
from jax.sharding import PartitionSpec as P

MESH = pl.DeviceIdType.MESH
BF16 = jnp.bfloat16
F32 = jnp.float32
NN = (((1,), (0,)), ((), ()))
NT = (((1,), (1,)), ((), ()))

MAIN, REM, WIDE = 512, 32, 640
ROWS = MAIN + REM
TWICE = ROWS + REM
DEEP = 2 * MAIN + 128


def halves(value):
    high = value.astype(BF16)
    return high, (value - high.astype(F32)).astype(BF16)


def dot(a, b, dims):
    return lax.dot_general(a, b, dims, preferred_element_type=F32)


def product(a, b):
    a_high, a_low = halves(a)
    b_high, b_low = halves(b)
    return dot(a_high, b_high, NN) + dot(a_high, b_low, NN) + dot(a_low, b_high, NN)


def stacked(rows):
    high = rows.astype(BF16).astype(F32)
    return jnp.concatenate([high, rows - high], axis=0).astype(BF16)


def times_block(rows, block):
    both = stacked(rows)
    high, low = halves(block)
    out = dot(both, high, NT) + dot(both, low, NT)
    return out[:8] + out[8:]


def step(rows, weights):
    both = stacked(rows)
    main = both[:, :MAIN]
    out = (
        dot(main, weights[:, :MAIN], NT)
        + dot(main, weights[:, MAIN : 2 * MAIN], NT)
        + dot(both[:, MAIN:], weights[:, 2 * MAIN :], NT)
    )
    return out[:8] + out[8:]


def pack_weights(weights, matrix):
    high, low = halves(matrix)
    last = matrix[:, MAIN:]
    last_high = last.astype(BF16).astype(F32)
    tail = (
        last_high + pltpu.roll(last - last_high, REM, 1) + pltpu.roll(last_high, 2 * REM, 1)
    ).astype(BF16)
    for columns, values in (
        (slice(0, MAIN), high[:, :MAIN]),
        (slice(MAIN, 2 * MAIN), low[:, :MAIN]),
        (slice(2 * MAIN, DEEP), tail),
    ):
        weights[:ROWS, columns] = values[:ROWS]
        weights[ROWS:TWICE, columns] = values[MAIN:ROWS]
    weights[TWICE:, :] = jnp.zeros((WIDE - TWICE, DEEP), BF16)


def put_block(matrix, target, source, block):
    row, col = 128 * target, 128 * source
    row_rem, col_rem = MAIN + 8 * target, MAIN + 8 * source
    matrix[row : row + 128, col : col + 128] = block[:128, :128]
    matrix[row : row + 128, col_rem : col_rem + 7] = block[:128, 128:]
    matrix[row_rem : row_rem + 7, col : col + 128] = block[128:, :128]
    matrix[row_rem : row_rem + 7, col_rem : col_rem + 7] = block[128:, 128:]


def put_rows(packed, element, rows):
    packed[:, 128 * element : 128 * element + 128] = rows[:, :128]
    packed[:, MAIN + 8 * element : MAIN + 8 * element + 7] = rows[:, 128:]
    packed[:, ROWS + 8 * element : ROWS + 8 * element + 7] = rows[:, 128:]


def kernel(
    flows,
    crosses,
    color_ref,
    rhs_hbm,
    old_hbm,
    inv_hbm,
    faces_hbm,
    out_ref,
    rhs,
    old,
    inv,
    faces,
    halo_left,
    halo_right,
    below,
    own,
    other,
    weights,
    pair_weights,
    offset,
    other_offset,
    arrived,
    leaving,
    load_sem,
    send_sem,
    recv_sem,
):
    flow, cross = lax.axis_index("flow"), lax.axis_index("cross")
    core = lax.rem(flow, 2)
    odd = core == 1
    has_left, has_right = cross > 0, cross < crosses - 1
    has_upper, has_lower = flow > 0, flow < flows - 1

    def at(flow_step, cross_step):
        return (flow + flow_step, cross + cross_step)

    barrier = pltpu.get_barrier_semaphore()
    partners = [
        (has_upper, at(-1, 0)),
        (has_lower, at(1, 0)),
        (has_left, at(0, -1)),
        (has_right, at(0, 1)),
        (odd & (flow >= 2), at(-2, 0)),
        (odd & (flow < flows - 2), at(2, 0)),
    ]
    expected = 0
    for present, device in partners:
        expected = expected + present.astype(jnp.int32)

        @pl.when(present)
        def _(device=device):
            pl.semaphore_signal(barrier, inc=1, device_id=device, device_id_type=MESH)

    def block_load(place, face, j, k):
        source = inv_hbm.at[0] if face is None else faces_hbm.at[0, face]
        target = inv if face is None else faces.at[face]
        return pltpu.make_async_copy(
            source.at[j, :, k, :], target.at[j, k], load_sem.at[place]
        )

    wanted = [(face, j, k) for face in (None, 0, 2, 3) for j in (0, 1) for k in (0, 1)]
    wanted += [(4, j, 1) for j in (0, 1)] + [(5, j, 0) for j in (0, 1)]
    wanted += [(1, j, k) for j in (0, 1) for k in (0, 1)]
    loads = [block_load(place, *block) for place, block in enumerate(wanted)]
    loads += [
        pltpu.make_async_copy(old_hbm.at[0], old, load_sem.at[len(wanted)]),
        pltpu.make_async_copy(rhs_hbm.at[0], rhs, load_sem.at[len(wanted) + 1]),
    ]
    for load in loads:
        load.start()

    own[...] = jnp.zeros_like(own)
    offset[...] = jnp.zeros_like(offset)
    pl.semaphore_wait(barrier, expected)

    def remote(source, target, place, device):
        return pltpu.make_async_remote_copy(
            src_ref=source,
            dst_ref=target,
            send_sem=send_sem.at[place],
            recv_sem=recv_sem.at[place],
            device_id=device,
            device_id_type=MESH,
        )

    halos = [
        (has_right, has_left, remote(old_hbm.at[0, 1], halo_left, 0, at(0, 1))),
        (has_left, has_right, remote(old_hbm.at[0, 0], halo_right, 1, at(0, -1))),
        (has_upper, has_lower, remote(old_hbm.at[0], below, 2, at(-1, 0))),
    ]
    for sends, _, halo in halos:
        pl.when(sends)(halo.start)

    even = color_ref[0, 0, 0] == 0

    def pick(first, second):
        return jnp.where(even, first, second)

    def cross_face(e):
        return faces[3 - e // 2, e // 2, e % 2]

    def span_face(e):
        return faces[5 - e % 2, e // 2, e % 2]

    def out_face(e):
        return faces[2 + e // 2, e // 2, e % 2]

    def inverse(e):
        return inv[e // 2, e % 2]

    for load in loads:
        load.wait()

    matrix = [
        remote(own.at[rows], other.at[rows], place, at(1, 0))
        for place, rows in (
            (3, pl.ds(0, 256)),
            (4, pl.ds(256, 256)),
            (5, pl.ds(MAIN, REM)),
        )
    ]

    @pl.when(has_upper)
    def _():
        diagonal = [-product(inverse(e), faces[0, e // 2, e % 2]) for e in range(4)]
        for e in range(4):
            put_block(own, e, e, diagonal[e])
        from_a, from_d = pick(diagonal[0], diagonal[1]), pick(diagonal[3], diagonal[2])
        inv_b, inv_c = pick(inverse(1), inverse(0)), pick(inverse(2), inverse(3))
        gain_bd = product(inv_b, pick(cross_face(1), cross_face(0)))
        gain_ba = product(inv_b, pick(span_face(1), span_face(0)))
        gain_ca = product(inv_c, pick(cross_face(2), cross_face(3)))
        gain_cd = product(inv_c, pick(span_face(2), span_face(3)))
        for source, gain, here, there in (
            (from_a, gain_ba, (1, 0), (0, 1)),
            (from_d, gain_bd, (1, 3), (0, 2)),
            (from_a, gain_ca, (2, 0), (3, 1)),
            (from_d, gain_cd, (2, 3), (3, 2)),
        ):
            block = -product(gain, source)
            nothing = jnp.zeros_like(block)
            put_block(own, *here, pick(block, nothing))
            put_block(own, *there, pick(nothing, block))

        @pl.when(core == 0)
        def _():
            for piece in matrix:
                piece.start()

        pack_weights(weights, own[...])

    for _, receives, halo in halos:
        pl.when(receives)(halo.wait_recv)

    def part(e):
        j, k = e // 2, e % 2
        halo = jnp.where(*((has_left, halo_left[k]) if j == 0 else (has_right, halo_right[k])), 0.0)
        under = jnp.where(has_lower, below[j, k], 0.0)
        return (
            rhs[j, k]
            - times_block(under, faces[1, j, k])
            - times_block(halo, out_face(e))
        )

    parts = [part(e) for e in range(4)]
    held = [old[e // 2, e % 2] for e in range(4)]
    old_b, old_c = pick(held[1], held[0]), pick(held[2], held[3])
    total_a = pick(parts[0], parts[1]) - (
        times_block(old_c, pick(cross_face(0), cross_face(1)))
        + times_block(old_b, pick(span_face(0), span_face(1)))
    )
    total_d = pick(parts[3], parts[2]) - (
        times_block(old_b, pick(cross_face(3), cross_face(2)))
        + times_block(old_c, pick(span_face(3), span_face(2)))
    )
    new_a = times_block(total_a, pick(inverse(0), inverse(1)))
    new_d = times_block(total_d, pick(inverse(3), inverse(2)))
    total_b = pick(parts[1], parts[0]) - (
        times_block(new_d, pick(cross_face(1), cross_face(0)))
        + times_block(new_a, pick(span_face(1), span_face(0)))
    )
    total_c = pick(parts[2], parts[3]) - (
        times_block(new_a, pick(cross_face(2), cross_face(3)))
        + times_block(new_d, pick(span_face(2), span_face(3)))
    )
    new_b = times_block(total_b, pick(inverse(1), inverse(0)))
    new_c = times_block(total_c, pick(inverse(2), inverse(3)))
    put_rows(offset, 0, pick(new_a, new_b))
    put_rows(offset, 1, pick(new_b, new_a))
    put_rows(offset, 2, pick(new_c, new_d))
    put_rows(offset, 3, pick(new_d, new_c))

    offset_copy = remote(offset, other_offset, 6, at(1, 0))
    to_other = remote(leaving, arrived, 7, at(1, 0))
    to_next = remote(leaving, arrived, 8, at(2, 0))

    def finish(rows):
        for e in range(4):
            out_ref[0, e // 2, e % 2, :, :128] = rows[:, 128 * e : 128 * e + 128]
            out_ref[0, e // 2, e % 2, :, 128:] = rows[:, MAIN + 8 * e : MAIN + 8 * e + 7]

    @pl.when(core == 0)
    def _():
        offset_copy.start()

        @pl.when(flow == 0)
        def _():
            finish(offset[...])

        @pl.when(has_upper)
        def _():
            to_other.wait_recv()
            finish(step(arrived[...], weights[...]) + offset[...])
            for piece in matrix:
                piece.wait_send()

        offset_copy.wait_send()

    @pl.when(odd)
    def _():
        @pl.when(flow == 1)
        def _():
            offset_copy.wait_recv()
            leaving[...] = step(other_offset[...], weights[...]) + offset[...]

        @pl.when(flow > 1)
        def _():
            left = weights.at[:TWICE]
            paired = jnp.zeros((TWICE, WIDE), F32)
            for half in (0, 1):
                matrix[half].wait_recv()
                here = slice(256 * half, 256 * half + 256)
                low_here = slice(MAIN + 256 * half, MAIN + 256 * half + 256)
                high, low = halves(other[here, :])
                paired = (
                    paired
                    + dot(left[:, here], high, NN)
                    + dot(left[:, here], low, NN)
                    + dot(left[:, low_here], high, NN)
                )
            matrix[2].wait_recv()
            high, low = halves(other[MAIN:, :])
            tail = jnp.concatenate([high, high, low, jnp.zeros_like(high)], axis=0)
            paired = paired + dot(left[:, 2 * MAIN :], tail, NN)
            pack_weights(pair_weights, paired)
            offset_copy.wait_recv()
            offset[...] = step(other_offset[...], weights[...]) + offset[...]
            to_next.wait_recv()
            leaving[...] = step(arrived[...], pair_weights[...]) + offset[...]

        @pl.when(has_lower)
        def _():
            to_next.start()
            to_other.start()

        finish(leaving[...])

        @pl.when(has_lower)
        def _():
            to_next.wait_send()
            to_other.wait_send()

    for sends, _, halo in halos:
        pl.when(sends)(halo.wait_send)


def body(flows, crosses, right_side, start_iterate, inverse_blocks, face_blocks, color_order):
    _, columns, spans, vectors, width = right_side.shape
    hbm = pl.BlockSpec(memory_space=pltpu.HBM)
    return pl.pallas_call(
        functools.partial(kernel, flows, crosses),
        out_shape=jax.ShapeDtypeStruct(right_side.shape, F32),
        in_specs=[pl.BlockSpec(memory_space=pltpu.SMEM), hbm, hbm, hbm, hbm],
        out_specs=pl.BlockSpec(memory_space=pltpu.VMEM),
        scratch_shapes=[
            pltpu.VMEM((columns, spans, vectors, width), F32),
            pltpu.VMEM((columns, spans, vectors, width), F32),
            pltpu.VMEM((columns, spans, width, width), F32),
            pltpu.VMEM((6, columns, spans, width, width), F32),
            pltpu.VMEM((spans, vectors, width), F32),
            pltpu.VMEM((spans, vectors, width), F32),
            pltpu.VMEM((columns, spans, vectors, width), F32),
            pltpu.VMEM((ROWS, WIDE), F32),
            pltpu.VMEM((ROWS, WIDE), F32),
            pltpu.VMEM((WIDE, DEEP), BF16),
            pltpu.VMEM((WIDE, DEEP), BF16),
            pltpu.VMEM((vectors, WIDE), F32),
            pltpu.VMEM((vectors, WIDE), F32),
            pltpu.VMEM((vectors, WIDE), F32),
            pltpu.VMEM((vectors, WIDE), F32),
            pltpu.SemaphoreType.DMA((26,)),
            pltpu.SemaphoreType.DMA((9,)),
            pltpu.SemaphoreType.DMA((9,)),
        ],
        compiler_params=pltpu.CompilerParams(
            collective_id=0, has_side_effects=True, vmem_limit_bytes=60 * 1024 * 1024
        ),
        cost_estimate=pl.CostEstimate(flops=10**9, bytes_accessed=4 * 10**6, transcendentals=0),
        name="sweep_chain",
    )(
        color_order,
        right_side,
        start_iterate,
        inverse_blocks.transpose(0, 1, 3, 2, 4),
        face_blocks.transpose(0, 1, 2, 4, 3, 5),
    )


def solution(mesh):
    return jax.shard_map(
        functools.partial(body, mesh.shape["flow"], mesh.shape["cross"]),
        mesh=mesh,
        in_specs=(
            P("flow", "cross", None, None, None),
            P("flow", "cross", None, None, None),
            P("flow", "cross", None, None, None),
            P("flow", None, "cross", None, None, None),
            P("flow", "cross", None),
        ),
        out_specs=P("flow", "cross", None, None, None),
        check_vma=False,
    )
```

```python
import functools

import jax
import jax.numpy as jnp
from jax import lax
from jax.experimental import pallas as pl
from jax.experimental.pallas import tpu as pltpu
from jax.sharding import PartitionSpec as P

MESH = pl.DeviceIdType.MESH
BF16 = jnp.bfloat16
F32 = jnp.float32
NN = (((1,), (0,)), ((), ()))
NT = (((1,), (1,)), ((), ()))

MAIN, REM, WIDE = 512, 32, 640
ROWS = MAIN + REM
TWICE = ROWS + REM
DEEP = 2 * MAIN + 128
EDGE, SIDE, FLAG, SENT = 1024, 1088, 1224, 1232
OWN, FIRST, CHIP, FAR, FAR_NEXT, SOME, ALL = range(7)
PLACES = (
    ((0, 2), (None, 4), (None, 5), None),
    ((4, None), (2, 0), None, (5, None)),
    ((6, None), None, (3, 1), (7, None)),
    (None, (None, 6), (None, 7), (1, 3)),
)


def halves(value):
    high = value.astype(BF16)
    return high, (value - high.astype(F32)).astype(BF16)


def dot(a, b, dims):
    return lax.dot_general(a, b, dims, preferred_element_type=F32)


def product(a, b):
    a_high, a_low = halves(a)
    b_high, b_low = halves(b)
    return dot(a_high, b_high, NN) + dot(a_high, b_low, NN) + dot(a_low, b_high, NN)


def stacked(rows):
    high = rows.astype(BF16).astype(F32)
    return jnp.concatenate([high, rows - high], axis=0).astype(BF16)


def times_block(rows, block):
    both = stacked(rows)
    high, low = halves(block)
    out = dot(both, high, NT) + dot(both, low, NT)
    return out[:8] + out[8:]


def step(rows, weights):
    both = stacked(rows)
    main = both[:, :MAIN]
    out = (
        dot(main, weights[:, :MAIN], NT)
        + dot(main, weights[:, MAIN : 2 * MAIN], NT)
        + dot(both[:, MAIN:], weights[:, 2 * MAIN :], NT)
    )
    return out[:8] + out[8:]


def fast_step(rows, weights):
    both = stacked(rows)
    main = both[:, :MAIN]
    out = (
        dot(main, weights[:MAIN], NN)
        + dot(main, weights[MAIN : 2 * MAIN], NN)
        + dot(both[:, MAIN:], weights[2 * MAIN :], NN)
    )
    return out[:8] + out[8:]


def pack_turned(weights, matrix):
    high, low = halves(matrix.T)
    weights[:MAIN] = high[:MAIN]
    weights[MAIN : 2 * MAIN] = low[:MAIN]
    weights[2 * MAIN : 2 * MAIN + REM] = high[MAIN:ROWS]
    weights[2 * MAIN + REM : 2 * MAIN + 2 * REM] = low[MAIN:ROWS]
    weights[2 * MAIN + 2 * REM :] = jnp.zeros((128 - 2 * REM, WIDE), BF16)


def pack_weights(weights, matrix):
    high, low = halves(matrix)
    last = matrix[:, MAIN:]
    last_high = last.astype(BF16).astype(F32)
    tail = (
        last_high + pltpu.roll(last - last_high, REM, 1) + pltpu.roll(last_high, 2 * REM, 1)
    ).astype(BF16)
    for columns, values in (
        (slice(0, MAIN), high[:, :MAIN]),
        (slice(MAIN, 2 * MAIN), low[:, :MAIN]),
        (slice(2 * MAIN, DEEP), tail),
    ):
        weights[:ROWS, columns] = values[:ROWS]
        weights[ROWS:TWICE, columns] = values[MAIN:ROWS]
    weights[TWICE:, :] = jnp.zeros((WIDE - TWICE, DEEP), BF16)


def composed(weights, later, earlier):
    pack_weights(weights, later)
    high, low = halves(earlier)
    tail_high, tail_low = high[MAIN:ROWS], low[MAIN:ROWS]
    tail = jnp.concatenate([tail_high, tail_high, tail_low, jnp.zeros_like(tail_high)], axis=0)
    return (
        dot(weights[:, :MAIN], high[:MAIN], NN)
        + dot(weights[:, :MAIN], low[:MAIN], NN)
        + dot(weights[:, MAIN : 2 * MAIN], high[:MAIN], NN)
        + dot(weights[:, 2 * MAIN :], tail, NN)
    )


def put_block(sent, place, block):
    sent[128 * place : 128 * place + 128] = block[:128, :128]
    sent[EDGE + 8 * place : EDGE + 8 * place + 7] = block[128:, :128]


def put_side(sent, target, source, block):
    lane = 32 * target + 8 * source
    sent[SIDE : SIDE + 135, lane : lane + 7] = block[:, 128:]


def spread(matrix, sent):
    even = sent[FLAG : FLAG + 1] > 0.5
    lanes = lax.broadcasted_iota(jnp.int32, (1, 128), 1)

    def fetch(places, start, height):
        if places is None:
            return jnp.zeros((height, 128), F32)
        first, second = (
            0.0 if place is None else sent[start + height * place : start + height * place + height]
            for place in places
        )
        return jnp.where(even, first, second)

    side = sent[SIDE:FLAG]
    for target, row in enumerate(PLACES):
        top, edge = slice(128 * target, 128 * target + 128), slice(MAIN + 8 * target, MAIN + 8 * target + 8)
        for source, places in enumerate(row):
            columns = slice(128 * source, 128 * source + 128)
            matrix[top, columns] = fetch(places, 0, 128)
            matrix[edge, columns] = fetch(places, EDGE, 8)
        turned = side if target == 0 else pltpu.roll(side, 128 - 32 * target, 1)
        turned = jnp.where(lanes < REM, turned, 0.0)
        matrix[top, MAIN:] = turned[:128]
        matrix[edge, MAIN:] = turned[128:]


def put_rows(packed, element, rows):
    packed[:, 128 * element : 128 * element + 128] = rows[:, :128]
    packed[:, MAIN + 8 * element : MAIN + 8 * element + 7] = rows[:, 128:]
    packed[:, ROWS + 8 * element : ROWS + 8 * element + 7] = rows[:, 128:]


def kernel(
    flows,
    crosses,
    color_ref,
    rhs_hbm,
    old_hbm,
    inv_hbm,
    faces_hbm,
    out_ref,
    rhs,
    old,
    inv,
    faces,
    halo_left,
    halo_right,
    below,
    sent,
    got,
    matrices,
    offsets,
    parts,
    weights,
    turned,
    arrived,
    leaving,
    load_sem,
    send_sem,
    recv_sem,
    order_sem,
):
    flow, cross = lax.axis_index("flow"), lax.axis_index("cross")
    core = lax.rem(flow, 2)
    odd = core == 1
    has_left, has_right = cross > 0, cross < crosses - 1
    has_upper, has_lower = flow > 0, flow < flows - 1
    inner = flow > 1

    def among(*layers):
        return functools.reduce(jnp.logical_or, [flow == layer for layer in layers])

    before, after = among(15, 19, 27, 30, 31), among(11, 21)
    one_more, two_more = among(11, 15), among(19, 21, 27, 30, 31)
    express = after
    helper = among(12, 13, 16, 17, 22, 23, 24, 25, 28, 29)
    goes_first, signals = among(12, 13, 17, 22, 25, 29), among(17, 22, 25, 29)
    goes_after = among(16, 23, 24, 28)
    to_site_step = jnp.where(
        among(12, 22), -1, jnp.where(flow == 23, -2, jnp.where(among(13, 17, 25, 29), 2, 3))
    )

    def at(flow_step, cross_step):
        return (flow + flow_step, cross + cross_step)

    barrier = pltpu.get_barrier_semaphore()
    partners = [
        (has_upper, at(-1, 0)),
        (has_lower, at(1, 0)),
        (has_left, at(0, -1)),
        (has_right, at(0, 1)),
        (odd & (flow >= 2), at(-2, 0)),
        (odd & (flow < flows - 2), at(2, 0)),
    ]
    for distance, layers in ((3, (16, 21, 24, 27, 28)), (4, (11, 15, 21, 27)), (6, (21,))):
        partners.append((among(*layers), at(distance, 0)))
        partners.append((among(*(layer + distance for layer in layers)), at(-distance, 0)))
    expected = 0
    for present, device in partners:
        expected = expected + present.astype(jnp.int32)

        @pl.when(present)
        def _(device=device):
            pl.semaphore_signal(barrier, inc=1, device_id=device, device_id_type=MESH)

    def block_load(place, face, j, k):
        source = inv_hbm.at[0] if face is None else faces_hbm.at[0, face]
        target = inv if face is None else faces.at[face]
        return pltpu.make_async_copy(
            source.at[j, :, k, :], target.at[j, k], load_sem.at[place]
        )

    cells = [(j, k) for j in (0, 1) for k in (0, 1)]
    span_blocks = [(4, 0, 1), (4, 1, 1), (5, 0, 0), (5, 1, 0)]
    groups = [
        [(None, *cell) for cell in cells],
        [(0, *cell) for cell in cells],
        span_blocks + [(face, *cell) for face in (2, 3) for cell in cells],
        [(1, *cell) for cell in cells],
    ]
    count, loads = 0, []
    for group in groups:
        loads.append([block_load(count + n, *block) for n, block in enumerate(group)])
        count += len(group)
    old_load = pltpu.make_async_copy(old_hbm.at[0], old, load_sem.at[count])
    rhs_load = pltpu.make_async_copy(rhs_hbm.at[0], rhs, load_sem.at[count + 1])
    old_load.start()
    rhs_load.start()

    @pl.when(inner)
    def _():
        for n in (0, 1, 2, 3):
            for load in loads[n]:
                load.start()

    @pl.when(~inner)
    def _():
        for n in (2, 3, 0, 1):
            for load in loads[n]:
                load.start()

    sent[...] = jnp.zeros_like(sent)
    offsets[OWN] = jnp.zeros((8, WIDE), F32)
    arrived[0] = jnp.zeros((8, WIDE), F32)
    for slot in (OWN, FIRST, FAR, FAR_NEXT):
        matrices[slot, ROWS:] = jnp.zeros((WIDE - ROWS, WIDE), F32)
    pl.semaphore_wait(barrier, expected)

    def remote(source, target, places, device):
        sending, receiving = places if isinstance(places, tuple) else (places, places)
        return pltpu.make_async_remote_copy(
            src_ref=source,
            dst_ref=target,
            send_sem=send_sem.at[sending],
            recv_sem=recv_sem.at[receiving],
            device_id=device,
            device_id_type=MESH,
        )

    halos = [
        (has_right, has_left, remote(old_hbm.at[0, 1], halo_left, 0, at(0, 1))),
        (has_left, has_right, remote(old_hbm.at[0, 0], halo_right, 1, at(0, -1))),
        (has_upper, has_lower, remote(old_hbm.at[0], below, 2, at(-1, 0))),
    ]
    for sends, _, halo in halos:
        pl.when(sends)(halo.start)

    even = color_ref[0, 0, 0] == 0

    def pick(first, second):
        return jnp.where(even, first, second)

    def cross_face(e):
        return faces[3 - e // 2, e // 2, e % 2]

    def span_face(e):
        return faces[5 - e % 2, e // 2, e % 2]

    def out_face(e):
        return faces[2 + e // 2, e // 2, e % 2]

    def inverse(e):
        return inv[e // 2, e % 2]

    for n in (0, 2):
        for load in loads[n]:
            load.wait()

    to_second = remote(sent, got.at[0], 3, at(1, 0))
    to_site = remote(sent, got.at[1 + core], 4 + core, at(to_site_step, 0))
    @pl.when(inner)
    def _():
        for load in loads[1]:
            load.wait()
        diagonal = [-product(inverse(e), faces[0, e // 2, e % 2]) for e in range(4)]
        from_a, from_d = pick(diagonal[0], diagonal[1]), pick(diagonal[3], diagonal[2])
        put_block(sent, 0, from_a)
        put_block(sent, 1, from_d)
        put_block(sent, 2, pick(diagonal[1], diagonal[0]))
        put_block(sent, 3, pick(diagonal[2], diagonal[3]))
        for e in range(4):
            put_side(sent, e, e, diagonal[e])
        inv_b, inv_c = pick(inverse(1), inverse(0)), pick(inverse(2), inverse(3))
        gain_ba = product(inv_b, pick(span_face(1), span_face(0)))
        gain_bd = product(inv_b, pick(cross_face(1), cross_face(0)))
        gain_ca = product(inv_c, pick(cross_face(2), cross_face(3)))
        gain_cd = product(inv_c, pick(span_face(2), span_face(3)))
        for slot, source, gain, here, there in (
            (4, from_a, gain_ba, (1, 0), (0, 1)),
            (5, from_d, gain_bd, (1, 3), (0, 2)),
            (6, from_a, gain_ca, (2, 0), (3, 1)),
            (7, from_d, gain_cd, (2, 3), (3, 2)),
        ):
            block = -product(gain, source)
            nothing = jnp.zeros_like(block)
            put_block(sent, slot, block)
            put_side(sent, *here, pick(block, nothing))
            put_side(sent, *there, pick(nothing, block))
        sent[FLAG:] = jnp.where(even, 1.0, 0.0) + jnp.zeros((8, 128), F32)
        pl.when(~odd)(to_second.start)
        pl.when(goes_first)(to_site.start)
        spread(matrices.at[OWN], sent)

    old_load.wait()
    rhs_load.wait()
    held = [old[e // 2, e % 2] for e in range(4)]
    old_b, old_c = pick(held[1], held[0]), pick(held[2], held[3])
    around_a = times_block(old_c, pick(cross_face(0), cross_face(1))) + times_block(
        old_b, pick(span_face(0), span_face(1))
    )
    around_d = times_block(old_b, pick(cross_face(3), cross_face(2))) + times_block(
        old_c, pick(span_face(3), span_face(2))
    )

    for load in loads[3]:
        load.wait()
    for _, receives, halo in halos:
        pl.when(receives)(halo.wait_recv)

    def part(e):
        j, k = e // 2, e % 2
        halo = jnp.where(*((has_left, halo_left[k]) if j == 0 else (has_right, halo_right[k])), 0.0)
        under = jnp.where(has_lower, below[j, k], 0.0)
        return (
            rhs[j, k]
            - times_block(under, faces[1, j, k])
            - times_block(halo, out_face(e))
        )

    for e in range(4):
        parts[e] = part(e)

    own_offset, first_offset = offsets.at[OWN], offsets.at[FIRST]
    offset_to_second = remote(own_offset, first_offset, 6, at(1, 0))
    offset_to_site = remote(own_offset, offsets.at[FAR + core], 7 + core, at(to_site_step, 0))

    @pl.when(flow == 1)
    def _():
        for load in loads[1]:
            load.wait()
        offset_to_second.wait_recv()
        for e in range(4):
            upper = jnp.concatenate(
                [
                    first_offset[:, 128 * e : 128 * e + 128],
                    first_offset[:, MAIN + 8 * e : MAIN + 8 * e + 7],
                ],
                axis=1,
            )
            parts[e] = parts[e] - times_block(upper, faces[0, e // 2, e % 2])

    total_a = pick(parts[0], parts[1]) - around_a
    total_d = pick(parts[3], parts[2]) - around_d
    new_a = times_block(total_a, pick(inverse(0), inverse(1)))
    new_d = times_block(total_d, pick(inverse(3), inverse(2)))
    total_b = pick(parts[1], parts[0]) - (
        times_block(new_d, pick(cross_face(1), cross_face(0)))
        + times_block(new_a, pick(span_face(1), span_face(0)))
    )
    total_c = pick(parts[2], parts[3]) - (
        times_block(new_a, pick(cross_face(2), cross_face(3)))
        + times_block(new_d, pick(span_face(2), span_face(3)))
    )
    new_b = times_block(total_b, pick(inverse(1), inverse(0)))
    new_c = times_block(total_c, pick(inverse(2), inverse(3)))
    put_rows(own_offset, 0, pick(new_a, new_b))
    put_rows(own_offset, 1, pick(new_b, new_a))
    put_rows(own_offset, 2, pick(new_c, new_d))
    put_rows(own_offset, 3, pick(new_d, new_c))

    pl.when(~odd)(offset_to_second.start)
    pl.when(helper)(offset_to_site.start)

    @pl.when(signals)
    def _():
        to_site.wait_send()
        pl.semaphore_signal(
            order_sem, inc=1, device_id=at(1 - 2 * core, 0), device_id_type=MESH
        )

    @pl.when(goes_after)
    def _():
        pl.semaphore_wait(order_sem, 1)
        to_site.start()

    def state(slot, send_place, flow_step):
        return remote(leaving.at[slot], arrived.at[1], (send_place, 9), at(flow_step, 0))

    sends = [
        (among(15, 27), state(1, 9, 4)),
        (flow == 27, state(1, 10, 3)),
        (odd & ~among(13, 17, 23, 25, 29, 31), state(1, 11, 2)),
        (odd & ~among(23, 29, 31), state(1, 12, 1)),
    ]
    express_sends = [
        (flow == 21, state(0, 13, 6)),
        (among(11, 21), state(0, 14, 4)),
        (flow == 21, state(0, 15, 3)),
    ]
    receives_state = sends[0][1].wait_recv

    def passed(box):
        return [
            remote(got.at[box], got.at[box], (15 + box, 3 + box), at(-1, 0)),
            remote(offsets.at[2 + box], offsets.at[2 + box], (17 + box, 6 + box), at(-1, 0)),
        ]

    @pl.when(~inner)
    def _():
        leaving[1] = own_offset[...]
        for present, copy in sends:
            pl.when(present)(copy.start)

    @pl.when(inner)
    def _():
        def compose(turn, carry):
            box = jnp.where(turn == 0, 0, jnp.where(after, turn, 3 - turn))
            layer = jnp.where(turn == 0, FIRST, 2 + box)
            held = jnp.where(turn == 0, OWN, jnp.where(turn == 1, jnp.where(odd, CHIP, OWN), SOME))
            result = jnp.where(turn == 0, CHIP, jnp.where(turn == 1, SOME, ALL))
            held_later = (turn == 0) | before
            later = jnp.where(held_later, held, layer)
            earlier = jnp.where(held_later, layer, held)
            remote(sent, got.at[box], (3, 3 + box), at(-1, 0)).wait_recv()
            remote(own_offset, offsets.at[layer], (6, 6 + box), at(-1, 0)).wait_recv()

            @pl.when((flow == flows - 1) & (turn > 0))
            def _():
                for copy in passed(box):
                    copy.start()

            spread(matrices.at[layer], got.at[box])
            matrices[result] = composed(weights, matrices[later], matrices[earlier])
            offsets[result] = step(offsets[earlier], weights[...]) + offsets[later]
            return carry

        more = jnp.where(two_more, 2, jnp.where(one_more, 1, 0))
        lax.fori_loop(1 - core, 1 + more, compose, 0)

        used = jnp.where(two_more, ALL, jnp.where(one_more, SOME, jnp.where(odd, CHIP, OWN)))
        pack_turned(turned.at[0], matrices[used])

        @pl.when(express)
        def _():
            pack_turned(turned.at[1], matrices[CHIP])

        turns = jnp.where(express, 3, 2)

        def advance(turn, carry):
            pl.when(turn == 1)(receives_state)
            last = turn == turns - 1
            own = express & last
            rows = arrived[jnp.where(turn == 0, 0, 1)]
            moved = fast_step(rows, turned.at[jnp.where(own, 1, 0)])
            leaving[jnp.where(last, 1, 0)] = moved + offsets[jnp.where(own, CHIP, used)]

            @pl.when(express & (turn == 1))
            def _():
                for present, copy in express_sends:
                    pl.when(present)(copy.start)

            @pl.when(last)
            def _():
                for present, copy in sends:
                    pl.when(present)(copy.start)

            return carry

        lax.fori_loop(0, turns, advance, 0)

    rows = leaving[1]
    for e in range(4):
        out_ref[0, e // 2, e % 2, :, :128] = rows[:, 128 * e : 128 * e + 128]
        out_ref[0, e // 2, e % 2, :, 128:] = rows[:, MAIN + 8 * e : MAIN + 8 * e + 7]

    for present, copy in sends:
        pl.when(present)(copy.wait_send)

    for present, copy in express_sends:
        pl.when(present)(copy.wait_send)

    @pl.when(flow == flows - 1)
    def _():
        for box in (1, 2):
            for copy in passed(box):
                copy.wait_send()

    @pl.when(flow == 0)
    def _():
        for load in loads[1]:
            load.wait()

    pl.when(inner & ~odd)(to_second.wait_send)
    pl.when(~odd)(offset_to_second.wait_send)
    pl.when(helper & ~signals)(to_site.wait_send)
    pl.when(helper)(offset_to_site.wait_send)
    for sends, _, halo in halos:
        pl.when(sends)(halo.wait_send)


def body(flows, crosses, right_side, start_iterate, inverse_blocks, face_blocks, color_order):
    _, columns, spans, vectors, width = right_side.shape
    hbm = pl.BlockSpec(memory_space=pltpu.HBM)
    return pl.pallas_call(
        functools.partial(kernel, flows, crosses),
        out_shape=jax.ShapeDtypeStruct(right_side.shape, F32),
        in_specs=[pl.BlockSpec(memory_space=pltpu.SMEM), hbm, hbm, hbm, hbm],
        out_specs=pl.BlockSpec(memory_space=pltpu.VMEM),
        scratch_shapes=[
            pltpu.VMEM((columns, spans, vectors, width), F32),
            pltpu.VMEM((columns, spans, vectors, width), F32),
            pltpu.VMEM((columns, spans, width, width), F32),
            pltpu.VMEM((6, columns, spans, width, width), F32),
            pltpu.VMEM((spans, vectors, width), F32),
            pltpu.VMEM((spans, vectors, width), F32),
            pltpu.VMEM((columns, spans, vectors, width), F32),
            pltpu.VMEM((SENT, 128), F32),
            pltpu.VMEM((3, SENT, 128), F32),
            pltpu.VMEM((7, WIDE, WIDE), F32),
            pltpu.VMEM((7, vectors, WIDE), F32),
            pltpu.VMEM((2 * columns, vectors, width), F32),
            pltpu.VMEM((WIDE, DEEP), BF16),
            pltpu.VMEM((2, DEEP, WIDE), BF16),
            pltpu.VMEM((2, vectors, WIDE), F32),
            pltpu.VMEM((2, vectors, WIDE), F32),
            pltpu.SemaphoreType.DMA((26,)),
            pltpu.SemaphoreType.DMA((20,)),
            pltpu.SemaphoreType.DMA((10,)),
            pltpu.SemaphoreType.REGULAR,
        ],
        compiler_params=pltpu.CompilerParams(
            collective_id=0, has_side_effects=True, vmem_limit_bytes=60 * 1024 * 1024
        ),
        cost_estimate=pl.CostEstimate(flops=10**9, bytes_accessed=4 * 10**6, transcendentals=0),
        name="sweep_chain",
    )(
        color_order,
        right_side,
        start_iterate,
        inverse_blocks.transpose(0, 1, 3, 2, 4),
        face_blocks.transpose(0, 1, 2, 4, 3, 5),
    )


def solution(mesh):
    return jax.shard_map(
        functools.partial(body, mesh.shape["flow"], mesh.shape["cross"]),
        mesh=mesh,
        in_specs=(
            P("flow", "cross", None, None, None),
            P("flow", "cross", None, None, None),
            P("flow", "cross", None, None, None),
            P("flow", None, "cross", None, None, None),
            P("flow", "cross", None),
        ),
        out_specs=P("flow", "cross", None, None, None),
        check_vma=False,
    )
```

```python
import functools

import jax
import jax.numpy as jnp
from jax import lax
from jax.experimental import pallas as pl
from jax.experimental.pallas import tpu as pltpu
from jax.sharding import PartitionSpec as P

MESH = pl.DeviceIdType.MESH
BF16 = jnp.bfloat16
F32 = jnp.float32
NN = (((1,), (0,)), ((), ()))
NT = (((1,), (1,)), ((), ()))

MAIN, REM, WIDE = 512, 32, 640
ROWS = MAIN + REM
TWICE = ROWS + REM
DEEP = 2 * MAIN + 128
EDGE, SIDE, FLAG, SENT = 1024, 1088, 1224, 1232
HALF = SENT // 2
OWN, FIRST, CHIP, FAR, MORE = 0, 1, 2, 3, 5
PLACES = (
    ((0, 2), (None, 4), (None, 5), None),
    ((4, None), (2, 0), None, (5, None)),
    ((6, None), None, (3, 1), (7, None)),
    (None, (None, 6), (None, 7), (1, 3)),
)


def halves(value):
    high = value.astype(BF16)
    return high, (value - high.astype(F32)).astype(BF16)


def dot(a, b, dims):
    return lax.dot_general(a, b, dims, preferred_element_type=F32)


def product(a, b):
    a_high, a_low = halves(a)
    b_high, b_low = halves(b)
    return dot(a_high, b_high, NN) + dot(a_high, b_low, NN) + dot(a_low, b_high, NN)


def stacked(rows):
    high = rows.astype(BF16).astype(F32)
    return jnp.concatenate([high, rows - high], axis=0).astype(BF16)


def times_halves(rows, high, low):
    both = stacked(rows)
    out = dot(both, high, NT) + dot(both, low, NT)
    return out[:8] + out[8:]


def times_block(rows, block):
    return times_halves(rows, *halves(block))


def step(rows, weights):
    both = stacked(rows)
    main = both[:, :MAIN]
    out = (
        dot(main, weights[:, :MAIN], NT)
        + dot(main, weights[:, MAIN : 2 * MAIN], NT)
        + dot(both[:, MAIN:], weights[:, 2 * MAIN :], NT)
    )
    return out[:8] + out[8:]


def fast_step(rows, weights):
    both = stacked(rows)
    main = both[:, :MAIN]
    out = (
        dot(main, weights[:MAIN], NN)
        + dot(main, weights[MAIN : 2 * MAIN], NN)
        + dot(both[:, MAIN:], weights[2 * MAIN :], NN)
    )
    return out[:8] + out[8:]


def pack_turned(weights, matrix):
    high, low = halves(matrix.T)
    weights[:MAIN] = high[:MAIN]
    weights[MAIN : 2 * MAIN] = low[:MAIN]
    weights[2 * MAIN : 2 * MAIN + REM] = high[MAIN:ROWS]
    weights[2 * MAIN + REM : 2 * MAIN + 2 * REM] = low[MAIN:ROWS]
    weights[2 * MAIN + 2 * REM :] = jnp.zeros((128 - 2 * REM, WIDE), BF16)


def pack_weights(weights, matrix):
    high, low = halves(matrix)
    last = matrix[:, MAIN:]
    last_high = last.astype(BF16).astype(F32)
    tail = (
        last_high + pltpu.roll(last - last_high, REM, 1) + pltpu.roll(last_high, 2 * REM, 1)
    ).astype(BF16)
    for columns, values in (
        (slice(0, MAIN), high[:, :MAIN]),
        (slice(MAIN, 2 * MAIN), low[:, :MAIN]),
        (slice(2 * MAIN, DEEP), tail),
    ):
        weights[:ROWS, columns] = values[:ROWS]
        weights[ROWS:TWICE, columns] = values[MAIN:ROWS]
    weights[TWICE:, :] = jnp.zeros((WIDE - TWICE, DEEP), BF16)


def composed(weights, later, earlier):
    pack_weights(weights, later)
    high, low = halves(earlier)
    tail_high, tail_low = high[MAIN:ROWS], low[MAIN:ROWS]
    tail = jnp.concatenate([tail_high, tail_high, tail_low, jnp.zeros_like(tail_high)], axis=0)
    return (
        dot(weights[:, :MAIN], high[:MAIN], NN)
        + dot(weights[:, :MAIN], low[:MAIN], NN)
        + dot(weights[:, MAIN : 2 * MAIN], high[:MAIN], NN)
        + dot(weights[:, 2 * MAIN :], tail, NN)
    )


def put_block(sent, place, block):
    sent[128 * place : 128 * place + 128] = block[:128, :128]
    sent[EDGE + 8 * place : EDGE + 8 * place + 7] = block[128:, :128]


def put_side(sent, target, source, block):
    lane = 32 * target + 8 * source
    sent[SIDE : SIDE + 135, lane : lane + 7] = block[:, 128:]


def spread(matrix, sent):
    even = sent[FLAG : FLAG + 1] > 0.5
    lanes = lax.broadcasted_iota(jnp.int32, (1, 128), 1)

    def fetch(places, start, height):
        if places is None:
            return jnp.zeros((height, 128), F32)
        first, second = (
            0.0 if place is None else sent[start + height * place : start + height * place + height]
            for place in places
        )
        return jnp.where(even, first, second)

    side = sent[SIDE:FLAG]
    for target, row in enumerate(PLACES):
        top, edge = slice(128 * target, 128 * target + 128), slice(MAIN + 8 * target, MAIN + 8 * target + 8)
        for source, places in enumerate(row):
            columns = slice(128 * source, 128 * source + 128)
            matrix[top, columns] = fetch(places, 0, 128)
            matrix[edge, columns] = fetch(places, EDGE, 8)
        turned = side if target == 0 else pltpu.roll(side, 128 - 32 * target, 1)
        turned = jnp.where(lanes < REM, turned, 0.0)
        matrix[top, MAIN:] = turned[:128]
        matrix[edge, MAIN:] = turned[128:]


def put_rows(packed, element, rows):
    packed[:, 128 * element : 128 * element + 128] = rows[:, :128]
    packed[:, MAIN + 8 * element : MAIN + 8 * element + 7] = rows[:, 128:]
    packed[:, ROWS + 8 * element : ROWS + 8 * element + 7] = rows[:, 128:]


def kernel(
    flows,
    crosses,
    color_ref,
    rhs_hbm,
    old_hbm,
    inv_hbm,
    faces_hbm,
    out_ref,
    rhs,
    old,
    inv,
    faces,
    halo_left,
    halo_right,
    below,
    sent,
    got,
    matrices,
    offsets,
    parts,
    blocks,
    weights,
    turned,
    arrived,
    leaving,
    load_sem,
    send_sem,
    recv_sem,
    order_sem,
):
    flow, cross = lax.axis_index("flow"), lax.axis_index("cross")
    core = lax.rem(flow, 2)
    odd = core == 1
    has_left, has_right = cross > 0, cross < crosses - 1
    has_upper, has_lower = flow > 0, flow < flows - 1
    inner = flow > 1

    def among(*layers):
        return functools.reduce(jnp.logical_or, [flow == layer for layer in layers])

    before, express = among(19, 26, 27, 30, 31), among(9, 13, 21)
    more = jnp.where(
        flow == 9, 1, jnp.where(flow == 19, 3, jnp.where(among(13, 21, 26, 27, 30, 31), 2, 0))
    )
    passes = among(27, 31)
    helper = among(10, 11, 14, 15, 16, 17, 22, 23, 24, 25, 28, 29)
    signals, goes_after = among(14, 17, 22, 25, 29), among(15, 16, 23, 24, 28)
    to_site_step = jnp.where(
        among(10, 14, 22),
        -1,
        jnp.where(flow == 23, -2, jnp.where(flow == 15, 4, jnp.where(odd, 2, 3))),
    )
    to_site_box = jnp.where(flow == 15, 3, 1 + core)

    def at(flow_step, cross_step):
        return (flow + flow_step, cross + cross_step)

    barrier = pltpu.get_barrier_semaphore()
    partners = [
        (has_upper, at(-1, 0)),
        (has_lower, at(1, 0)),
        (has_left, at(0, -1)),
        (has_right, at(0, 1)),
        (odd & (flow >= 2), at(-2, 0)),
        (odd & (flow < flows - 2), at(2, 0)),
    ]
    for distance, layers in (
        (3, (16, 21, 24, 27, 28)),
        (4, (9, 15, 21, 27)),
        (5, (21,)),
        (6, (13, 21)),
    ):
        partners.append((among(*layers), at(distance, 0)))
        partners.append((among(*(layer + distance for layer in layers)), at(-distance, 0)))
    expected = 0
    for present, device in partners:
        expected = expected + present.astype(jnp.int32)

        @pl.when(present)
        def _(device=device):
            pl.semaphore_signal(barrier, inc=1, device_id=device, device_id_type=MESH)

    def block_load(place, face, j, k):
        source = inv_hbm.at[0] if face is None else faces_hbm.at[0, face]
        target = inv if face is None else faces.at[face]
        return pltpu.make_async_copy(
            source.at[j, :, k, :], target.at[j, k], load_sem.at[place]
        )

    cells = [(j, k) for j in (0, 1) for k in (0, 1)]
    span_blocks = [(4, 0, 1), (4, 1, 1), (5, 0, 0), (5, 1, 0)]
    groups = [
        [(None, *cell) for cell in cells],
        [(0, *cell) for cell in cells],
        span_blocks + [(face, *cell) for face in (2, 3) for cell in cells],
        [(1, *cell) for cell in cells],
    ]
    count, loads = 0, []
    for group in groups:
        loads.append([block_load(count + n, *block) for n, block in enumerate(group)])
        count += len(group)
    old_load = pltpu.make_async_copy(old_hbm.at[0], old, load_sem.at[count])
    rhs_load = pltpu.make_async_copy(rhs_hbm.at[0], rhs, load_sem.at[count + 1])
    old_load.start()
    rhs_load.start()

    @pl.when(inner)
    def _():
        for n in (0, 1, 2, 3):
            for load in loads[n]:
                load.start()

    @pl.when(~inner)
    def _():
        for n in (2, 3, 0, 1):
            for load in loads[n]:
                load.start()

    sent[...] = jnp.zeros_like(sent)
    offsets[OWN] = jnp.zeros((8, WIDE), F32)
    arrived[0] = jnp.zeros((8, WIDE), F32)
    for slot in (OWN, FIRST, FAR, FAR + 1, FAR + 2):
        matrices[slot, ROWS:] = jnp.zeros((WIDE - ROWS, WIDE), F32)
    pl.semaphore_wait(barrier, expected)

    def remote(source, target, places, device):
        sending, receiving = places if isinstance(places, tuple) else (places, places)
        return pltpu.make_async_remote_copy(
            src_ref=source,
            dst_ref=target,
            send_sem=send_sem.at[sending],
            recv_sem=recv_sem.at[receiving],
            device_id=device,
            device_id_type=MESH,
        )

    halos = [
        (has_right, has_left, remote(old_hbm.at[0, 1], halo_left, 0, at(0, 1))),
        (has_left, has_right, remote(old_hbm.at[0, 0], halo_right, 1, at(0, -1))),
        (has_upper, has_lower, remote(old_hbm.at[0], below, 2, at(-1, 0))),
    ]
    for sends, _, halo in halos:
        pl.when(sends)(halo.start)

    even = color_ref[0, 0, 0] == 0

    def pick(first, second):
        return jnp.where(even, first, second)

    def cross_face(e):
        return faces[3 - e // 2, e // 2, e % 2]

    def span_face(e):
        return faces[5 - e % 2, e // 2, e % 2]

    def out_face(e):
        return faces[2 + e // 2, e // 2, e % 2]

    def inverse(e):
        return inv[e // 2, e % 2]

    for n in (0, 2):
        for load in loads[n]:
            load.wait()

    def in_halves(source, target, places, box, flow_step):
        return [
            remote(
                source.at[pl.ds(HALF * n, HALF)],
                target.at[pl.ds(HALF * n, HALF)],
                (places + n, (3, 12)[n] + box),
                at(flow_step, 0),
            )
            for n in (0, 1)
        ]

    to_second = in_halves(sent, got.at[0], 3, 0, 1)
    to_site = in_halves(sent, got.at[to_site_box], 5, to_site_box, to_site_step)

    @pl.when(inner)
    def _():
        for load in loads[1]:
            load.wait()
        diagonal = [-product(inverse(e), faces[0, e // 2, e % 2]) for e in range(4)]
        from_a, from_d = pick(diagonal[0], diagonal[1]), pick(diagonal[3], diagonal[2])
        put_block(sent, 0, from_a)
        put_block(sent, 1, from_d)
        put_block(sent, 2, pick(diagonal[1], diagonal[0]))
        put_block(sent, 3, pick(diagonal[2], diagonal[3]))
        for e in range(4):
            put_side(sent, e, e, diagonal[e])
        inv_b, inv_c = pick(inverse(1), inverse(0)), pick(inverse(2), inverse(3))
        gain_ba = product(inv_b, pick(span_face(1), span_face(0)))
        gain_bd = product(inv_b, pick(cross_face(1), cross_face(0)))
        gain_ca = product(inv_c, pick(cross_face(2), cross_face(3)))
        gain_cd = product(inv_c, pick(span_face(2), span_face(3)))
        for slot, source, gain, here, there in (
            (4, from_a, gain_ba, (1, 0), (0, 1)),
            (5, from_d, gain_bd, (1, 3), (0, 2)),
            (6, from_a, gain_ca, (2, 0), (3, 1)),
            (7, from_d, gain_cd, (2, 3), (3, 2)),
        ):
            block = -product(gain, source)
            nothing = jnp.zeros_like(block)
            put_block(sent, slot, block)
            put_side(sent, *here, pick(block, nothing))
            put_side(sent, *there, pick(nothing, block))
        sent[FLAG:] = jnp.where(even, 1.0, 0.0) + jnp.zeros((8, 128), F32)
        for copy in to_second:
            pl.when(~odd)(copy.start)
        for copy in to_site:
            pl.when(helper & ~goes_after)(copy.start)
        spread(matrices.at[OWN], sent)
        matrices[OWN, ROWS:TWICE] = matrices[OWN, MAIN:ROWS]

    old_load.wait()
    rhs_load.wait()
    held = [old[e // 2, e % 2] for e in range(4)]
    old_b, old_c = pick(held[1], held[0]), pick(held[2], held[3])
    around_a = times_block(old_c, pick(cross_face(0), cross_face(1))) + times_block(
        old_b, pick(span_face(0), span_face(1))
    )
    around_d = times_block(old_b, pick(cross_face(3), cross_face(2))) + times_block(
        old_c, pick(span_face(3), span_face(2))
    )

    for load in loads[3]:
        load.wait()

    for e in range(4):
        blocks[2 * e, 0], blocks[2 * e, 1] = halves(faces[1, e // 2, e % 2])
        blocks[2 * e + 1, 0], blocks[2 * e + 1, 1] = halves(out_face(e))
    for n, block in enumerate(
        (
            pick(inverse(0), inverse(1)),
            pick(inverse(3), inverse(2)),
            pick(cross_face(1), cross_face(0)),
            pick(span_face(1), span_face(0)),
            pick(cross_face(2), cross_face(3)),
            pick(span_face(2), span_face(3)),
            pick(inverse(1), inverse(0)),
            pick(inverse(2), inverse(3)),
        )
    ):
        blocks[8 + n, 0], blocks[8 + n, 1] = halves(block)

    def times(rows, n):
        return times_halves(rows, blocks[n, 0], blocks[n, 1])

    for _, receives, halo in halos:
        pl.when(receives)(halo.wait_recv)

    def part(e):
        j, k = e // 2, e % 2
        halo = jnp.where(*((has_left, halo_left[k]) if j == 0 else (has_right, halo_right[k])), 0.0)
        under = jnp.where(has_lower, below[j, k], 0.0)
        return (
            rhs[j, k]
            - times(under, 2 * e)
            - times(halo, 2 * e + 1)
        )

    for e in range(4):
        parts[e] = part(e)

    own_offset, first_offset = offsets.at[OWN], offsets.at[FIRST]
    offset_to_second = remote(own_offset, first_offset, (7, 7), at(1, 0))
    offset_to_site = remote(
        own_offset, offsets.at[2 + to_site_box], (8, 7 + to_site_box), at(to_site_step, 0)
    )

    @pl.when(flow == 1)
    def _():
        for load in loads[1]:
            load.wait()
        offset_to_second.wait_recv()
        for e in range(4):
            upper = jnp.concatenate(
                [
                    first_offset[:, 128 * e : 128 * e + 128],
                    first_offset[:, MAIN + 8 * e : MAIN + 8 * e + 7],
                ],
                axis=1,
            )
            parts[e] = parts[e] - times_block(upper, faces[0, e // 2, e % 2])

    total_a = pick(parts[0], parts[1]) - around_a
    total_d = pick(parts[3], parts[2]) - around_d
    new_a, new_d = times(total_a, 8), times(total_d, 9)
    total_b = pick(parts[1], parts[0]) - (times(new_d, 10) + times(new_a, 11))
    total_c = pick(parts[2], parts[3]) - (times(new_a, 12) + times(new_d, 13))
    new_b, new_c = times(total_b, 14), times(total_c, 15)
    put_rows(own_offset, 0, pick(new_a, new_b))
    put_rows(own_offset, 1, pick(new_b, new_a))
    put_rows(own_offset, 2, pick(new_c, new_d))
    put_rows(own_offset, 3, pick(new_d, new_c))

    pl.when(~odd)(offset_to_second.start)
    pl.when(helper)(offset_to_site.start)

    @pl.when(signals)
    def _():
        to_site[0].wait_send()
        pl.semaphore_signal(
            order_sem, inc=1, device_id=at(1 - 2 * core, 0), device_id_type=MESH
        )

    @pl.when(goes_after)
    def _():
        pl.semaphore_wait(order_sem, 1)
        for copy in to_site:
            copy.start()

    def state(slot, send_place, flow_step):
        return remote(leaving.at[slot], arrived.at[1], (send_place, 11), at(flow_step, 0))

    sends = [
        (flow == 27, state(1, 9, 4)),
        (flow == 27, state(1, 10, 3)),
        (odd & ~among(11, 13, 17, 23, 25, 29, 31), state(1, 11, 2)),
        (odd & ~among(23, 25, 29, 31), state(1, 12, 1)),
    ]
    express_sends = [
        (among(13, 21), state(0, 13, 6)),
        (flow == 21, state(0, 14, 5)),
        (among(9, 21), state(0, 15, 4)),
        (flow == 21, state(0, 16, 3)),
        (flow == 13, state(0, 17, 2)),
    ]
    receives_state = sends[0][1].wait_recv

    def passed(box):
        offset = remote(offsets.at[2 + box], offsets.at[2 + box], (17 + box, 7 + box), at(-1, 0))
        return in_halves(got.at[box], got.at[box], 18 + 2 * box, box, -1) + [offset]

    @pl.when(~inner)
    def _():
        leaving[1] = own_offset[...]
        for present, copy in sends:
            pl.when(present)(copy.start)

    @pl.when(inner)
    def _():
        base = jnp.where(odd, CHIP, OWN)

        def compose(turn, carry):
            box = jnp.where(
                (turn == 0) | (turn == 3) | among(9, 21), turn, 3 - turn
            )
            layer = jnp.where(turn == 0, FIRST, 2 + box)
            held = jnp.where(turn == 0, OWN, jnp.where(turn == 1, base, MORE - 1 + turn))
            result = jnp.where(turn == 0, CHIP, MORE + turn)
            held_later = (turn == 0) | before | ((flow == 13) & (turn == 1))
            later = jnp.where(held_later, held, layer)
            earlier = jnp.where(held_later, layer, held)
            for copy in in_halves(sent, got.at[box], 3, box, -1):
                copy.wait_recv()
            remote(own_offset, offsets.at[layer], (7, 7 + box), at(-1, 0)).wait_recv()

            @pl.when(passes & (turn > 0))
            def _():
                for copy in passed(box):
                    copy.start()

            spread(matrices.at[layer], got.at[box])
            matrices[result] = composed(weights, matrices[later], matrices[earlier])
            offsets[result] = step(offsets[earlier], weights[...]) + offsets[later]
            return carry

        lax.fori_loop(1 - core, 1 + more, compose, 0)

        own_used = jnp.where(flow == 13, MORE + 1, CHIP)
        used = jnp.where(more > 0, MORE + more, jnp.where(odd & (flow != 15), CHIP, OWN))
        pack_turned(turned.at[0], matrices[used])

        @pl.when(express)
        def _():
            pack_turned(turned.at[1], matrices[own_used])

        turns = jnp.where(express, 3, 2)

        def advance(turn, carry):
            pl.when(turn == 1)(receives_state)
            last = turn == turns - 1
            own = express & last
            rows = arrived[jnp.where(turn == 0, 0, 1)]
            moved = fast_step(rows, turned.at[jnp.where(own, 1, 0)])
            leaving[jnp.where(last, 1, 0)] = moved + offsets[jnp.where(own, own_used, used)]

            @pl.when(express & (turn == 1))
            def _():
                for present, copy in express_sends:
                    pl.when(present)(copy.start)

            @pl.when(last)
            def _():
                for present, copy in sends:
                    pl.when(present)(copy.start)

            return carry

        lax.fori_loop(0, turns, advance, 0)

    rows = leaving[1]
    for e in range(4):
        out_ref[0, e // 2, e % 2, :, :128] = rows[:, 128 * e : 128 * e + 128]
        out_ref[0, e // 2, e % 2, :, 128:] = rows[:, MAIN + 8 * e : MAIN + 8 * e + 7]

    for present, copy in sends:
        pl.when(present)(copy.wait_send)

    for present, copy in express_sends:
        pl.when(present)(copy.wait_send)

    @pl.when(passes)
    def _():
        for box in (1, 2):
            for copy in passed(box):
                copy.wait_send()

    @pl.when(flow == 0)
    def _():
        for load in loads[1]:
            load.wait()

    for copy in to_second:
        pl.when(inner & ~odd)(copy.wait_send)
    pl.when(~odd)(offset_to_second.wait_send)
    pl.when(helper & ~signals)(to_site[0].wait_send)
    pl.when(helper)(to_site[1].wait_send)
    pl.when(helper)(offset_to_site.wait_send)
    for sends, _, halo in halos:
        pl.when(sends)(halo.wait_send)


def body(flows, crosses, right_side, start_iterate, inverse_blocks, face_blocks, color_order):
    _, columns, spans, vectors, width = right_side.shape
    hbm = pl.BlockSpec(memory_space=pltpu.HBM)
    return pl.pallas_call(
        functools.partial(kernel, flows, crosses),
        out_shape=jax.ShapeDtypeStruct(right_side.shape, F32),
        in_specs=[pl.BlockSpec(memory_space=pltpu.SMEM), hbm, hbm, hbm, hbm],
        out_specs=pl.BlockSpec(memory_space=pltpu.VMEM),
        scratch_shapes=[
            pltpu.VMEM((columns, spans, vectors, width), F32),
            pltpu.VMEM((columns, spans, vectors, width), F32),
            pltpu.VMEM((columns, spans, width, width), F32),
            pltpu.VMEM((6, columns, spans, width, width), F32),
            pltpu.VMEM((spans, vectors, width), F32),
            pltpu.VMEM((spans, vectors, width), F32),
            pltpu.VMEM((columns, spans, vectors, width), F32),
            pltpu.VMEM((SENT, 128), F32),
            pltpu.VMEM((4, SENT, 128), F32),
            pltpu.VMEM((9, WIDE, WIDE), F32),
            pltpu.VMEM((9, vectors, WIDE), F32),
            pltpu.VMEM((2 * columns, vectors, width), F32),
            pltpu.VMEM((16, 2, width, width), BF16),
            pltpu.VMEM((WIDE, DEEP), BF16),
            pltpu.VMEM((2, DEEP, WIDE), BF16),
            pltpu.VMEM((2, vectors, WIDE), F32),
            pltpu.VMEM((2, vectors, WIDE), F32),
            pltpu.SemaphoreType.DMA((26,)),
            pltpu.SemaphoreType.DMA((24,)),
            pltpu.SemaphoreType.DMA((16,)),
            pltpu.SemaphoreType.REGULAR,
        ],
        compiler_params=pltpu.CompilerParams(
            collective_id=0, has_side_effects=True, vmem_limit_bytes=60 * 1024 * 1024
        ),
        cost_estimate=pl.CostEstimate(flops=10**9, bytes_accessed=4 * 10**6, transcendentals=0),
        name="sweep_chain",
    )(
        color_order,
        right_side,
        start_iterate,
        inverse_blocks.transpose(0, 1, 3, 2, 4),
        face_blocks.transpose(0, 1, 2, 4, 3, 5),
    )


def solution(mesh):
    return jax.shard_map(
        functools.partial(body, mesh.shape["flow"], mesh.shape["cross"]),
        mesh=mesh,
        in_specs=(
            P("flow", "cross", None, None, None),
            P("flow", "cross", None, None, None),
            P("flow", "cross", None, None, None),
            P("flow", None, "cross", None, None, None),
            P("flow", "cross", None),
        ),
        out_specs=P("flow", "cross", None, None, None),
        check_vma=False,
    )
```

```python
import functools

import jax
import jax.numpy as jnp
from jax import lax
from jax.experimental import pallas as pl
from jax.experimental.pallas import tpu as pltpu
from jax.sharding import PartitionSpec as P

MESH = pl.DeviceIdType.MESH
BF16 = jnp.bfloat16
F32 = jnp.float32
NN = (((1,), (0,)), ((), ()))
NT = (((1,), (1,)), ((), ()))

MAIN, REM, WIDE = 512, 32, 640
ROWS = MAIN + REM
TWICE = ROWS + REM
DEEP = 2 * MAIN + 128
EDGE, SIDE, FLAG, SENT = 1024, 1088, 1224, 1248
PARTS = 4
PART = SENT // PARTS
OWN, FIRST, CHIP, FAR, MORE = 0, 1, 2, 3, 5
PLACES = (
    ((0, 2), (None, 4), (None, 5), None),
    ((4, None), (2, 0), None, (5, None)),
    ((6, None), None, (3, 1), (7, None)),
    (None, (None, 6), (None, 7), (1, 3)),
)


def halves(value):
    high = value.astype(BF16)
    return high, (value - high.astype(F32)).astype(BF16)


def dot(a, b, dims):
    return lax.dot_general(a, b, dims, preferred_element_type=F32)


def product(a, b):
    a_high, a_low = halves(a)
    b_high, b_low = halves(b)
    return dot(a_high, b_high, NN) + dot(a_high, b_low, NN) + dot(a_low, b_high, NN)


def stacked(rows):
    high = rows.astype(BF16).astype(F32)
    return jnp.concatenate([high, rows - high], axis=0).astype(BF16)


def times_halves(rows, high, low):
    both = stacked(rows)
    out = dot(both, high, NT) + dot(both, low, NT)
    return out[:8] + out[8:]


def times_block(rows, block):
    return times_halves(rows, *halves(block))


def step(rows, weights):
    both = stacked(rows)
    main = both[:, :MAIN]
    out = (
        dot(main, weights[:, :MAIN], NT)
        + dot(main, weights[:, MAIN : 2 * MAIN], NT)
        + dot(both[:, MAIN:], weights[:, 2 * MAIN :], NT)
    )
    return out[:8] + out[8:]


def fast_step(rows, weights):
    both = stacked(rows)
    main = both[:, :MAIN]
    out = (
        dot(main, weights[:MAIN], NN)
        + dot(main, weights[MAIN : 2 * MAIN], NN)
        + dot(both[:, MAIN:], weights[2 * MAIN :], NN)
    )
    return out[:8] + out[8:]


def pack_turned(weights, matrix):
    high, low = halves(matrix.T)
    weights[:MAIN] = high[:MAIN]
    weights[MAIN : 2 * MAIN] = low[:MAIN]
    weights[2 * MAIN : 2 * MAIN + REM] = high[MAIN:ROWS]
    weights[2 * MAIN + REM : 2 * MAIN + 2 * REM] = low[MAIN:ROWS]
    weights[2 * MAIN + 2 * REM :] = jnp.zeros((128 - 2 * REM, WIDE), BF16)


def pack_weights(weights, matrix):
    high, low = halves(matrix)
    last = matrix[:, MAIN:]
    last_high = last.astype(BF16).astype(F32)
    tail = (
        last_high + pltpu.roll(last - last_high, REM, 1) + pltpu.roll(last_high, 2 * REM, 1)
    ).astype(BF16)
    for columns, values in (
        (slice(0, MAIN), high[:, :MAIN]),
        (slice(MAIN, 2 * MAIN), low[:, :MAIN]),
        (slice(2 * MAIN, DEEP), tail),
    ):
        weights[:ROWS, columns] = values[:ROWS]
        weights[ROWS:TWICE, columns] = values[MAIN:ROWS]
    weights[TWICE:, :] = jnp.zeros((WIDE - TWICE, DEEP), BF16)


def composed(weights, later, earlier):
    pack_weights(weights, later)
    high, low = halves(earlier)
    tail_high, tail_low = high[MAIN:ROWS], low[MAIN:ROWS]
    tail = jnp.concatenate([tail_high, tail_high, tail_low, jnp.zeros_like(tail_high)], axis=0)
    return (
        dot(weights[:, :MAIN], high[:MAIN], NN)
        + dot(weights[:, :MAIN], low[:MAIN], NN)
        + dot(weights[:, MAIN : 2 * MAIN], high[:MAIN], NN)
        + dot(weights[:, 2 * MAIN :], tail, NN)
    )


def put_block(sent, place, block):
    sent[128 * place : 128 * place + 128] = block[:128, :128]
    sent[EDGE + 8 * place : EDGE + 8 * place + 7] = block[128:, :128]


def put_side(sent, target, source, block):
    lane = 32 * target + 8 * source
    sent[SIDE : SIDE + 135, lane : lane + 7] = block[:, 128:]


def spread(matrix, sent):
    even = sent[FLAG : FLAG + 1] > 0.5
    lanes = lax.broadcasted_iota(jnp.int32, (1, 128), 1)

    def fetch(places, start, height):
        if places is None:
            return jnp.zeros((height, 128), F32)
        first, second = (
            0.0 if place is None else sent[start + height * place : start + height * place + height]
            for place in places
        )
        return jnp.where(even, first, second)

    side = sent[SIDE:FLAG]
    for target, row in enumerate(PLACES):
        top, edge = slice(128 * target, 128 * target + 128), slice(MAIN + 8 * target, MAIN + 8 * target + 8)
        for source, places in enumerate(row):
            columns = slice(128 * source, 128 * source + 128)
            matrix[top, columns] = fetch(places, 0, 128)
            matrix[edge, columns] = fetch(places, EDGE, 8)
        turned = side if target == 0 else pltpu.roll(side, 128 - 32 * target, 1)
        turned = jnp.where(lanes < REM, turned, 0.0)
        matrix[top, MAIN:] = turned[:128]
        matrix[edge, MAIN:] = turned[128:]


def put_rows(packed, element, rows):
    packed[:, 128 * element : 128 * element + 128] = rows[:, :128]
    packed[:, MAIN + 8 * element : MAIN + 8 * element + 7] = rows[:, 128:]
    packed[:, ROWS + 8 * element : ROWS + 8 * element + 7] = rows[:, 128:]


def kernel(
    flows,
    crosses,
    color_ref,
    rhs_hbm,
    old_hbm,
    inv_hbm,
    faces_hbm,
    out_ref,
    rhs,
    old,
    inv,
    faces,
    halo_left,
    halo_right,
    below,
    sent,
    got,
    matrices,
    offsets,
    parts,
    blocks,
    weights,
    turned,
    arrived,
    leaving,
    load_sem,
    send_sem,
    recv_sem,
    order_sem,
):
    flow, cross = lax.axis_index("flow"), lax.axis_index("cross")
    core = lax.rem(flow, 2)
    odd = core == 1
    has_left, has_right = cross > 0, cross < crosses - 1
    has_upper, has_lower = flow > 0, flow < flows - 1
    inner = flow > 1

    def among(*layers):
        return functools.reduce(jnp.logical_or, [flow == layer for layer in layers])

    before, express = among(19, 26, 27, 30, 31), among(9, 13, 21)
    more = jnp.where(
        flow == 9, 1, jnp.where(flow == 13, 3, jnp.where(among(19, 21, 26, 27, 30, 31), 2, 0))
    )
    passes = among(27, 31)
    helper = among(10, 11, 14, 15, 16, 17, 22, 23, 24, 25, 28, 29)
    signals, goes_after = among(22, 25, 29), among(23, 24, 28)
    to_site_step = jnp.where(
        among(10, 14, 22),
        -1,
        jnp.where(among(15, 23), -2, jnp.where(odd, 2, 3)),
    )
    relayed, relays = among(15, 16), among(4, 10)
    to_site_box = jnp.where(flow == 15, 3, 1 + core)

    def at(flow_step, cross_step):
        return (flow + flow_step, cross + cross_step)

    barrier = pltpu.get_barrier_semaphore()
    partners = [
        (has_upper, at(-1, 0)),
        (has_lower, at(1, 0)),
        (has_left, at(0, -1)),
        (has_right, at(0, 1)),
        (odd & (flow >= 2), at(-2, 0)),
        (odd & (flow < flows - 2), at(2, 0)),
    ]
    for distance, layers in (
        (3, (13, 16, 21, 24, 27, 28)),
        (4, (9, 13, 21, 27)),
        (5, (21,)),
        (6, (10, 13, 21)),
        (9, (4, 10)),
        (11, (4,)),
    ):
        partners.append((among(*layers), at(distance, 0)))
        partners.append((among(*(layer + distance for layer in layers)), at(-distance, 0)))
    expected = 0
    for present, device in partners:
        expected = expected + present.astype(jnp.int32)

        @pl.when(present)
        def _(device=device):
            pl.semaphore_signal(barrier, inc=1, device_id=device, device_id_type=MESH)

    def block_load(place, face, j, k):
        source = inv_hbm.at[0] if face is None else faces_hbm.at[0, face]
        target = inv if face is None else faces.at[face]
        return pltpu.make_async_copy(
            source.at[j, :, k, :], target.at[j, k], load_sem.at[place]
        )

    cells = [(j, k) for j in (0, 1) for k in (0, 1)]
    span_blocks = [(4, 0, 1), (4, 1, 1), (5, 0, 0), (5, 1, 0)]
    groups = [
        [(None, *cell) for cell in cells],
        [(0, *cell) for cell in cells],
        span_blocks + [(face, *cell) for face in (2, 3) for cell in cells],
        [(1, *cell) for cell in cells],
    ]
    count, loads = 0, []
    for group in groups:
        loads.append([block_load(count + n, *block) for n, block in enumerate(group)])
        count += len(group)
    old_load = pltpu.make_async_copy(old_hbm.at[0], old, load_sem.at[count])
    rhs_load = pltpu.make_async_copy(rhs_hbm.at[0], rhs, load_sem.at[count + 1])
    old_load.start()
    rhs_load.start()

    @pl.when(inner)
    def _():
        for n in (0, 1, 2, 3):
            for load in loads[n]:
                load.start()

    @pl.when(~inner)
    def _():
        for n in (2, 3, 0, 1):
            for load in loads[n]:
                load.start()

    sent[...] = jnp.zeros_like(sent)
    offsets[OWN] = jnp.zeros((8, WIDE), F32)
    arrived[0] = jnp.zeros((8, WIDE), F32)
    for slot in (OWN, FIRST, FAR, FAR + 1, FAR + 2):
        matrices[slot, ROWS:] = jnp.zeros((WIDE - ROWS, WIDE), F32)
    pl.semaphore_wait(barrier, expected)

    def remote(source, target, places, device):
        sending, receiving = places if isinstance(places, tuple) else (places, places)
        return pltpu.make_async_remote_copy(
            src_ref=source,
            dst_ref=target,
            send_sem=send_sem.at[sending],
            recv_sem=recv_sem.at[receiving],
            device_id=device,
            device_id_type=MESH,
        )

    halos = [
        (has_right, has_left, remote(old_hbm.at[0, 1], halo_left, 0, at(0, 1))),
        (has_left, has_right, remote(old_hbm.at[0, 0], halo_right, 1, at(0, -1))),
        (has_upper, has_lower, remote(old_hbm.at[0], below, 2, at(-1, 0))),
    ]
    for sends, _, halo in halos:
        pl.when(sends)(halo.start)

    even = color_ref[0, 0, 0] == 0

    def pick(first, second):
        return jnp.where(even, first, second)

    def cross_face(e):
        return faces[3 - e // 2, e // 2, e % 2]

    def span_face(e):
        return faces[5 - e % 2, e // 2, e % 2]

    def out_face(e):
        return faces[2 + e // 2, e // 2, e % 2]

    def inverse(e):
        return inv[e // 2, e % 2]

    def in_parts(source, target, sending, receiving, flow_step):
        return [
            remote(
                source.at[pl.ds(PART * n, PART)],
                target.at[pl.ds(PART * n, PART)],
                (sending + n, receiving + n),
                at(flow_step, 0),
            )
            for n in range(PARTS)
        ]

    def received(box):
        return 3 + PARTS * box

    to_second = in_parts(sent, got.at[0], 3, received(0), 1)
    to_site = in_parts(
        sent,
        got.at[jnp.where(relayed, 1, to_site_box)],
        7,
        jnp.where(relayed, 24, received(to_site_box)),
        jnp.where(flow == 15, -11, jnp.where(flow == 16, -6, to_site_step)),
    )
    relay_box = jnp.where(flow == 4, 3, 1)
    to_relay = in_parts(sent, got.at[1], 32, 24, -1)
    relay = in_parts(got.at[1], got.at[relay_box], 32, received(relay_box), 9)

    @pl.when(~inner)
    def _():
        for n in (0, 2):
            for load in loads[n]:
                load.wait()

    @pl.when(inner)
    def _():
        for n in (0, 1):
            for load in loads[n]:
                load.wait()
        diagonal = [-product(inverse(e), faces[0, e // 2, e % 2]) for e in range(4)]
        from_a, from_d = pick(diagonal[0], diagonal[1]), pick(diagonal[3], diagonal[2])
        put_block(sent, 0, from_a)
        put_block(sent, 1, from_d)
        put_block(sent, 2, pick(diagonal[1], diagonal[0]))
        put_block(sent, 3, pick(diagonal[2], diagonal[3]))
        for e in range(4):
            put_side(sent, e, e, diagonal[e])
        for load in loads[2]:
            load.wait()
        inv_b, inv_c = pick(inverse(1), inverse(0)), pick(inverse(2), inverse(3))
        gain_ba = product(inv_b, pick(span_face(1), span_face(0)))
        gain_bd = product(inv_b, pick(cross_face(1), cross_face(0)))
        gain_ca = product(inv_c, pick(cross_face(2), cross_face(3)))
        gain_cd = product(inv_c, pick(span_face(2), span_face(3)))
        for slot, source, gain, here, there in (
            (4, from_a, gain_ba, (1, 0), (0, 1)),
            (5, from_d, gain_bd, (1, 3), (0, 2)),
            (6, from_a, gain_ca, (2, 0), (3, 1)),
            (7, from_d, gain_cd, (2, 3), (3, 2)),
        ):
            block = -product(gain, source)
            nothing = jnp.zeros_like(block)
            put_block(sent, slot, block)
            put_side(sent, *here, pick(block, nothing))
            put_side(sent, *there, pick(nothing, block))
        sent[FLAG:] = jnp.where(even, 1.0, 0.0) + jnp.zeros((SENT - FLAG, 128), F32)
        for copy in to_site:
            pl.when(helper & ~goes_after)(copy.start)
        for copy in to_second:
            pl.when(~odd)(copy.start)
        spread(matrices.at[OWN], sent)
        matrices[OWN, ROWS:TWICE] = matrices[OWN, MAIN:ROWS]

    old_load.wait()
    rhs_load.wait()
    held = [old[e // 2, e % 2] for e in range(4)]
    old_b, old_c = pick(held[1], held[0]), pick(held[2], held[3])
    around_a = times_block(old_c, pick(cross_face(0), cross_face(1))) + times_block(
        old_b, pick(span_face(0), span_face(1))
    )
    around_d = times_block(old_b, pick(cross_face(3), cross_face(2))) + times_block(
        old_c, pick(span_face(3), span_face(2))
    )

    for load in loads[3]:
        load.wait()

    for e in range(4):
        blocks[2 * e, 0], blocks[2 * e, 1] = halves(faces[1, e // 2, e % 2])
        blocks[2 * e + 1, 0], blocks[2 * e + 1, 1] = halves(out_face(e))
    for n, block in enumerate(
        (
            pick(inverse(0), inverse(1)),
            pick(inverse(3), inverse(2)),
            pick(cross_face(1), cross_face(0)),
            pick(span_face(1), span_face(0)),
            pick(cross_face(2), cross_face(3)),
            pick(span_face(2), span_face(3)),
            pick(inverse(1), inverse(0)),
            pick(inverse(2), inverse(3)),
        )
    ):
        blocks[8 + n, 0], blocks[8 + n, 1] = halves(block)

    def times(rows, n):
        return times_halves(rows, blocks[n, 0], blocks[n, 1])

    for _, receives, halo in halos:
        pl.when(receives)(halo.wait_recv)

    def part(e):
        j, k = e // 2, e % 2
        halo = jnp.where(*((has_left, halo_left[k]) if j == 0 else (has_right, halo_right[k])), 0.0)
        under = jnp.where(has_lower, below[j, k], 0.0)
        return (
            rhs[j, k]
            - times(under, 2 * e)
            - times(halo, 2 * e + 1)
        )

    for e in range(4):
        parts[e] = part(e)

    own_offset, first_offset = offsets.at[OWN], offsets.at[FIRST]
    offset_to_second = remote(own_offset, first_offset, (11, 19), at(1, 0))
    offset_to_site = remote(
        own_offset, offsets.at[2 + to_site_box], (12, 19 + to_site_box), at(to_site_step, 0)
    )

    @pl.when(flow == 1)
    def _():
        for load in loads[1]:
            load.wait()
        offset_to_second.wait_recv()
        for e in range(4):
            upper = jnp.concatenate(
                [
                    first_offset[:, 128 * e : 128 * e + 128],
                    first_offset[:, MAIN + 8 * e : MAIN + 8 * e + 7],
                ],
                axis=1,
            )
            parts[e] = parts[e] - times_block(upper, faces[0, e // 2, e % 2])

    total_a = pick(parts[0], parts[1]) - around_a
    total_d = pick(parts[3], parts[2]) - around_d
    new_a, new_d = times(total_a, 8), times(total_d, 9)
    total_b = pick(parts[1], parts[0]) - (times(new_d, 10) + times(new_a, 11))
    total_c = pick(parts[2], parts[3]) - (times(new_a, 12) + times(new_d, 13))
    new_b, new_c = times(total_b, 14), times(total_c, 15)
    put_rows(own_offset, 0, pick(new_a, new_b))
    put_rows(own_offset, 1, pick(new_b, new_a))
    put_rows(own_offset, 2, pick(new_c, new_d))
    put_rows(own_offset, 3, pick(new_d, new_c))

    pl.when(~odd)(offset_to_second.start)
    pl.when(helper)(offset_to_site.start)

    @pl.when(signals)
    def _():
        for copy in to_site[:2]:
            copy.wait_send()
        pl.semaphore_signal(
            order_sem, inc=1, device_id=at(1 - 2 * core, 0), device_id_type=MESH
        )

    @pl.when(goes_after)
    def _():
        pl.semaphore_wait(order_sem, 1)
        for copy in to_site:
            copy.start()

    @pl.when(relays)
    def _():
        for arriving, onward in zip(to_relay, relay):
            arriving.wait_recv()
            onward.start()

    def state(slot, send_place, flow_step):
        return remote(leaving.at[slot], arrived.at[1], (send_place, 23), at(flow_step, 0))

    sends = [
        (flow == 27, state(1, 13, 4)),
        (flow == 27, state(1, 14, 3)),
        (odd & ~among(11, 15, 17, 23, 25, 29, 31), state(1, 15, 2)),
        (odd & ~among(15, 23, 25, 29, 31), state(1, 16, 1)),
    ]
    express_sends = [
        (among(13, 21), state(0, 17, 6)),
        (flow == 21, state(0, 18, 5)),
        (express, state(0, 19, 4)),
        (among(13, 21), state(0, 20, 3)),
    ]
    receives_state = sends[0][1].wait_recv

    def passed(box):
        first = 17 + 5 * box
        offset = offsets.at[2 + box]
        return in_parts(got.at[box], got.at[box], first, received(box), -1) + [
            remote(offset, offset, (first + PARTS, 19 + box), at(-1, 0))
        ]

    @pl.when(~inner)
    def _():
        leaving[1] = own_offset[...]
        for present, copy in sends:
            pl.when(present)(copy.start)

    @pl.when(inner)
    def _():
        base = jnp.where(odd, CHIP, OWN)
        own_used = jnp.where(flow == 13, MORE + 1, CHIP)

        def compose(turn, carry):
            box = jnp.where(
                (turn == 0) | (turn == 3) | among(9, 21), turn, 3 - turn
            )
            layer = jnp.where(turn == 0, FIRST, 2 + box)
            held = jnp.where(turn == 0, OWN, jnp.where(turn == 1, base, MORE - 1 + turn))
            result = jnp.where(turn == 0, CHIP, MORE + turn)
            held_later = (turn == 0) | before | ((flow == 13) & (turn == 1))
            later = jnp.where(held_later, held, layer)
            earlier = jnp.where(held_later, layer, held)

            @pl.when(express & (turn == more))
            def _():
                pack_turned(turned.at[1], matrices[own_used])

            for copy in in_parts(sent, got.at[box], 3, received(box), -1):
                copy.wait_recv()
            remote(own_offset, offsets.at[layer], (11, 19 + box), at(-1, 0)).wait_recv()

            @pl.when(passes & (turn > 0))
            def _():
                for copy in passed(box):
                    copy.start()

            spread(matrices.at[layer], got.at[box])
            matrices[result] = composed(weights, matrices[later], matrices[earlier])
            offsets[result] = step(offsets[earlier], weights[...]) + offsets[later]
            return carry

        lax.fori_loop(1 - core, 1 + more, compose, 0)

        used = jnp.where(more > 0, MORE + more, base)
        pack_turned(turned.at[0], matrices[used])

        turns = jnp.where(express, 3, 2)

        def advance(turn, carry):
            pl.when(turn == 1)(receives_state)
            last = turn == turns - 1
            own = express & last
            rows = arrived[jnp.where(turn == 0, 0, 1)]
            moved = fast_step(rows, turned.at[jnp.where(own, 1, 0)])
            leaving[jnp.where(last, 1, 0)] = moved + offsets[jnp.where(own, own_used, used)]

            @pl.when(express & (turn == 1))
            def _():
                for present, copy in express_sends:
                    pl.when(present)(copy.start)

            @pl.when(last)
            def _():
                for present, copy in sends:
                    pl.when(present)(copy.start)

            return carry

        lax.fori_loop(0, turns, advance, 0)

    rows = leaving[1]
    for e in range(4):
        out_ref[0, e // 2, e % 2, :, :128] = rows[:, 128 * e : 128 * e + 128]
        out_ref[0, e // 2, e % 2, :, 128:] = rows[:, MAIN + 8 * e : MAIN + 8 * e + 7]

    for present, copy in sends:
        pl.when(present)(copy.wait_send)

    for present, copy in express_sends:
        pl.when(present)(copy.wait_send)

    @pl.when(passes)
    def _():
        for box in (1, 2):
            for copy in passed(box):
                copy.wait_send()

    @pl.when(flow == 0)
    def _():
        for load in loads[1]:
            load.wait()

    for copy in to_second:
        pl.when(inner & ~odd)(copy.wait_send)
    pl.when(~odd)(offset_to_second.wait_send)
    for n, copy in enumerate(to_site):
        pl.when(helper & ~signals if n < 2 else helper)(copy.wait_send)
    for copy in relay:
        pl.when(relays)(copy.wait_send)
    pl.when(helper)(offset_to_site.wait_send)
    for sends, _, halo in halos:
        pl.when(sends)(halo.wait_send)


def body(flows, crosses, right_side, start_iterate, inverse_blocks, face_blocks, color_order):
    _, columns, spans, vectors, width = right_side.shape
    hbm = pl.BlockSpec(memory_space=pltpu.HBM)
    return pl.pallas_call(
        functools.partial(kernel, flows, crosses),
        out_shape=jax.ShapeDtypeStruct(right_side.shape, F32),
        in_specs=[pl.BlockSpec(memory_space=pltpu.SMEM), hbm, hbm, hbm, hbm],
        out_specs=pl.BlockSpec(memory_space=pltpu.VMEM),
        scratch_shapes=[
            pltpu.VMEM((columns, spans, vectors, width), F32),
            pltpu.VMEM((columns, spans, vectors, width), F32),
            pltpu.VMEM((columns, spans, width, width), F32),
            pltpu.VMEM((6, columns, spans, width, width), F32),
            pltpu.VMEM((spans, vectors, width), F32),
            pltpu.VMEM((spans, vectors, width), F32),
            pltpu.VMEM((columns, spans, vectors, width), F32),
            pltpu.VMEM((SENT, 128), F32),
            pltpu.VMEM((4, SENT, 128), F32),
            pltpu.VMEM((9, WIDE, WIDE), F32),
            pltpu.VMEM((9, vectors, WIDE), F32),
            pltpu.VMEM((2 * columns, vectors, width), F32),
            pltpu.VMEM((16, 2, width, width), BF16),
            pltpu.VMEM((WIDE, DEEP), BF16),
            pltpu.VMEM((2, DEEP, WIDE), BF16),
            pltpu.VMEM((2, vectors, WIDE), F32),
            pltpu.VMEM((2, vectors, WIDE), F32),
            pltpu.SemaphoreType.DMA((26,)),
            pltpu.SemaphoreType.DMA((36,)),
            pltpu.SemaphoreType.DMA((28,)),
            pltpu.SemaphoreType.REGULAR,
        ],
        compiler_params=pltpu.CompilerParams(
            collective_id=0, has_side_effects=True, vmem_limit_bytes=60 * 1024 * 1024
        ),
        cost_estimate=pl.CostEstimate(flops=10**9, bytes_accessed=4 * 10**6, transcendentals=0),
        name="sweep_chain",
    )(
        color_order,
        right_side,
        start_iterate,
        inverse_blocks.transpose(0, 1, 3, 2, 4),
        face_blocks.transpose(0, 1, 2, 4, 3, 5),
    )


def solution(mesh):
    return jax.shard_map(
        functools.partial(body, mesh.shape["flow"], mesh.shape["cross"]),
        mesh=mesh,
        in_specs=(
            P("flow", "cross", None, None, None),
            P("flow", "cross", None, None, None),
            P("flow", "cross", None, None, None),
            P("flow", None, "cross", None, None, None),
            P("flow", "cross", None),
        ),
        out_specs=P("flow", "cross", None, None, None),
        check_vma=False,
    )
```

```python
import functools

import jax
import jax.numpy as jnp
from jax import lax
from jax.experimental import pallas as pl
from jax.experimental.pallas import tpu as pltpu
from jax.sharding import PartitionSpec as P

MESH = pl.DeviceIdType.MESH
BF16 = jnp.bfloat16
F32 = jnp.float32
NN = (((1,), (0,)), ((), ()))
NT = (((1,), (1,)), ((), ()))

MAIN, REM, WIDE = 512, 32, 640
ROWS = MAIN + REM
TWICE = ROWS + REM
DEEP = 2 * MAIN + 128
EDGE, SIDE, FLAG, SENT = 1024, 1088, 1224, 1248
PARTS = 4
PART = SENT // PARTS
OWN, FIRST, CHIP, FAR, MORE = 0, 1, 2, 3, 6
PLACES = (
    ((0, 2), (None, 4), (None, 5), None),
    ((4, None), (2, 0), None, (5, None)),
    ((6, None), None, (3, 1), (7, None)),
    (None, (None, 6), (None, 7), (1, 3)),
)


def halves(value):
    high = value.astype(BF16)
    return high, (value - high.astype(F32)).astype(BF16)


def dot(a, b, dims):
    return lax.dot_general(a, b, dims, preferred_element_type=F32)


def product(a, b):
    a_high, a_low = halves(a)
    b_high, b_low = halves(b)
    return dot(a_high, b_high, NN) + dot(a_high, b_low, NN) + dot(a_low, b_high, NN)


def stacked(rows):
    high = rows.astype(BF16).astype(F32)
    return jnp.concatenate([high, rows - high], axis=0).astype(BF16)


def times_block(rows, block):
    both = stacked(rows)
    high, low = halves(block)
    out = dot(both, high, NT) + dot(both, low, NT)
    return out[:8] + out[8:]


def step(rows, weights):
    both = stacked(rows)
    main = both[:, :MAIN]
    out = (
        dot(main, weights[:, :MAIN], NT)
        + dot(main, weights[:, MAIN : 2 * MAIN], NT)
        + dot(both[:, MAIN:], weights[:, 2 * MAIN :], NT)
    )
    return out[:8] + out[8:]


def fast_step(rows, weights):
    both = stacked(rows)
    main = both[:, :MAIN]
    out = (
        dot(main, weights[:MAIN], NN)
        + dot(main, weights[MAIN : 2 * MAIN], NN)
        + dot(both[:, MAIN:], weights[2 * MAIN :], NN)
    )
    return out[:8] + out[8:]


def pack_turned(weights, matrix):
    high, low = halves(matrix.T)
    weights[:MAIN] = high[:MAIN]
    weights[MAIN : 2 * MAIN] = low[:MAIN]
    weights[2 * MAIN : 2 * MAIN + REM] = high[MAIN:ROWS]
    weights[2 * MAIN + REM : 2 * MAIN + 2 * REM] = low[MAIN:ROWS]
    weights[2 * MAIN + 2 * REM :] = jnp.zeros((128 - 2 * REM, WIDE), BF16)


def pack_weights(weights, matrix):
    high, low = halves(matrix)
    last = matrix[:, MAIN:]
    last_high = last.astype(BF16).astype(F32)
    tail = (
        last_high + pltpu.roll(last - last_high, REM, 1) + pltpu.roll(last_high, 2 * REM, 1)
    ).astype(BF16)
    for columns, values in (
        (slice(0, MAIN), high[:, :MAIN]),
        (slice(MAIN, 2 * MAIN), low[:, :MAIN]),
        (slice(2 * MAIN, DEEP), tail),
    ):
        weights[:ROWS, columns] = values[:ROWS]
        weights[ROWS:TWICE, columns] = values[MAIN:ROWS]
    weights[TWICE:, :] = jnp.zeros((WIDE - TWICE, DEEP), BF16)


def composed(weights, later, earlier):
    pack_weights(weights, later)
    high, low = halves(earlier)
    tail_high, tail_low = high[MAIN:ROWS], low[MAIN:ROWS]
    tail = jnp.concatenate([tail_high, tail_high, tail_low, jnp.zeros_like(tail_high)], axis=0)
    return (
        dot(weights[:, :MAIN], high[:MAIN], NN)
        + dot(weights[:, :MAIN], low[:MAIN], NN)
        + dot(weights[:, MAIN : 2 * MAIN], high[:MAIN], NN)
        + dot(weights[:, 2 * MAIN :], tail, NN)
    )


def put_block(sent, place, block):
    sent[128 * place : 128 * place + 128] = block[:128, :128]
    sent[EDGE + 8 * place : EDGE + 8 * place + 7] = block[128:, :128]


def put_side(sent, target, source, block):
    lane = 32 * target + 8 * source
    sent[SIDE : SIDE + 135, lane : lane + 7] = block[:, 128:]


def spread(matrix, sent):
    even = sent[FLAG : FLAG + 1] > 0.5
    lanes = lax.broadcasted_iota(jnp.int32, (1, 128), 1)

    def fetch(places, start, height):
        if places is None:
            return jnp.zeros((height, 128), F32)
        first, second = (
            0.0 if place is None else sent[start + height * place : start + height * place + height]
            for place in places
        )
        return jnp.where(even, first, second)

    side = sent[SIDE:FLAG]
    for target, row in enumerate(PLACES):
        top, edge = slice(128 * target, 128 * target + 128), slice(MAIN + 8 * target, MAIN + 8 * target + 8)
        for source, places in enumerate(row):
            columns = slice(128 * source, 128 * source + 128)
            matrix[top, columns] = fetch(places, 0, 128)
            matrix[edge, columns] = fetch(places, EDGE, 8)
        turned = side if target == 0 else pltpu.roll(side, 128 - 32 * target, 1)
        turned = jnp.where(lanes < REM, turned, 0.0)
        matrix[top, MAIN:] = turned[:128]
        matrix[edge, MAIN:] = turned[128:]


def put_rows(packed, element, rows):
    packed[:, 128 * element : 128 * element + 128] = rows[:, :128]
    packed[:, MAIN + 8 * element : MAIN + 8 * element + 7] = rows[:, 128:]
    packed[:, ROWS + 8 * element : ROWS + 8 * element + 7] = rows[:, 128:]


def kernel(
    flows,
    crosses,
    color_hbm,
    rhs_hbm,
    old_hbm,
    inv_hbm,
    faces_hbm,
    out_ref,
    colors,
    rhs,
    old,
    inv,
    faces,
    halo_left,
    halo_right,
    below,
    sent,
    got,
    matrices,
    offsets,
    parts,
    weights,
    turned,
    arrived,
    leaving,
    load_sem,
    send_sem,
    recv_sem,
    order_sem,
):
    flow, cross = lax.axis_index("flow"), lax.axis_index("cross")
    core = lax.rem(flow, 2)
    odd = core == 1
    has_left, has_right = cross > 0, cross < crosses - 1
    has_upper, has_lower = flow > 0, flow < flows - 1
    inner = flow > 1

    def among(*layers):
        return functools.reduce(jnp.logical_or, [flow == layer for layer in layers])

    before, express = among(26, 27, 30, 31), among(9, 13, 19)
    more = jnp.where(
        flow == 9,
        1,
        jnp.where(
            flow == 13, 3, jnp.where(among(19, 27), 4, jnp.where(among(26, 30, 31), 2, 0))
        ),
    )
    passes = among(27, 31)
    helper = among(10, 11, 14, 15, 16, 17, 20, 21, 22, 23, 24, 25, 28, 29)
    signals, goes_after = among(20, 23, 25, 29), among(21, 22, 24, 28)
    to_site_step = jnp.where(
        among(10, 14, 20),
        -1,
        jnp.where(
            among(15, 21),
            -2,
            jnp.where(flow == 22, 5, jnp.where(flow == 23, 4, jnp.where(odd, 2, 3))),
        ),
    )
    to_site_box = jnp.where(among(15, 20, 23), 3, jnp.where(among(21, 22), 4, 1 + core))
    relayed, relays = among(15, 16), among(4, 10)

    def at(flow_step, cross_step):
        return (flow + flow_step, cross + cross_step)

    barrier = pltpu.get_barrier_semaphore()
    partners = [
        (has_upper, at(-1, 0)),
        (has_lower, at(1, 0)),
        (has_left, at(0, -1)),
        (has_right, at(0, 1)),
        (odd & (flow >= 2), at(-2, 0)),
        (odd & (flow < flows - 2), at(2, 0)),
    ]
    for distance, layers in (
        (3, (13, 16, 19, 23, 24, 27, 28)),
        (4, (9, 13, 19, 23, 27)),
        (5, (22,)),
        (6, (10, 13)),
        (8, (19,)),
        (9, (4, 10)),
        (11, (4,)),
    ):
        partners.append((among(*layers), at(distance, 0)))
        partners.append((among(*(layer + distance for layer in layers)), at(-distance, 0)))

    def block_load(place, face, j, k):
        source = inv_hbm.at[0] if face is None else faces_hbm.at[0, face]
        target = inv if face is None else faces.at[face]
        return pltpu.make_async_copy(
            source.at[j, :, k, :], target.at[j, k], load_sem.at[place]
        )

    cells = [(j, k) for j in (0, 1) for k in (0, 1)]
    span_blocks = [(4, 0, 1), (4, 1, 1), (5, 0, 0), (5, 1, 0)]
    groups = [
        [(None, *cell) for cell in cells],
        [(0, *cell) for cell in cells],
        span_blocks + [(face, *cell) for face in (2, 3) for cell in cells],
        [(1, *cell) for cell in cells],
    ]
    count, loads = 0, []
    for group in groups:
        loads.append([block_load(count + n, *block) for n, block in enumerate(group)])
        count += len(group)
    old_load = pltpu.make_async_copy(old_hbm.at[0], old, load_sem.at[count])
    rhs_load = pltpu.make_async_copy(rhs_hbm.at[0], rhs, load_sem.at[count + 1])
    color_load = pltpu.make_async_copy(color_hbm.at[0], colors, load_sem.at[count + 2])
    color_load.start()
    old_load.start()
    rhs_load.start()

    @pl.when(inner)
    def _():
        for n in (0, 1, 2, 3):
            for load in loads[n]:
                load.start()

    @pl.when(~inner)
    def _():
        for n in (2, 3, 0, 1):
            for load in loads[n]:
                load.start()

    expected = 0
    for present, device in partners:
        expected = expected + present.astype(jnp.int32)

        @pl.when(present)
        def _(device=device):
            pl.semaphore_signal(barrier, inc=1, device_id=device, device_id_type=MESH)

    offsets[OWN] = jnp.zeros((8, WIDE), F32)
    arrived[0] = jnp.zeros((8, WIDE), F32)
    pl.semaphore_wait(barrier, expected)

    def remote(source, target, places, device):
        sending, receiving = places if isinstance(places, tuple) else (places, places)
        return pltpu.make_async_remote_copy(
            src_ref=source,
            dst_ref=target,
            send_sem=send_sem.at[sending],
            recv_sem=recv_sem.at[receiving],
            device_id=device,
            device_id_type=MESH,
        )

    halos = [
        (has_right, has_left, remote(old_hbm.at[0, 1], halo_left, 0, at(0, 1))),
        (has_left, has_right, remote(old_hbm.at[0, 0], halo_right, 1, at(0, -1))),
        (has_upper, has_lower, remote(old_hbm.at[0], below, 2, at(-1, 0))),
    ]
    for sends, _, halo in halos:
        pl.when(sends)(halo.start)

    color_load.wait()
    even = colors[0, 0] == 0

    def pick(first, second):
        return jnp.where(even, first, second)

    def cross_face(e):
        return faces[3 - e // 2, e // 2, e % 2]

    def span_face(e):
        return faces[5 - e % 2, e // 2, e % 2]

    def out_face(e):
        return faces[2 + e // 2, e // 2, e % 2]

    def inverse(e):
        return inv[e // 2, e % 2]

    def in_parts(source, target, sending, receiving, flow_step):
        return [
            remote(
                source.at[pl.ds(PART * n, PART)],
                target.at[pl.ds(PART * n, PART)],
                (sending + n, receiving + n),
                at(flow_step, 0),
            )
            for n in range(PARTS)
        ]

    def received(box):
        return 3 + PARTS * box

    to_second = in_parts(sent, got.at[0], 3, received(0), 1)
    to_site = in_parts(
        sent,
        got.at[jnp.where(relayed, 1, to_site_box)],
        7,
        jnp.where(relayed, 29, received(to_site_box)),
        jnp.where(flow == 15, -11, jnp.where(flow == 16, -6, to_site_step)),
    )
    relay_box = jnp.where(flow == 4, 3, 1)
    to_relay = in_parts(sent, got.at[1], 32, 29, -1)
    relay = in_parts(got.at[1], got.at[relay_box], 32, received(relay_box), 9)

    @pl.when(~inner)
    def _():
        for load in loads[2]:
            load.wait()

    @pl.when(inner)
    def _():
        sent[...] = jnp.zeros_like(sent)
        for slot in (OWN, FIRST, FAR, FAR + 1, FAR + 2, FAR + 3):
            matrices[slot, ROWS:] = jnp.zeros((WIDE - ROWS, WIDE), F32)
        for n in (0, 1):
            for load in loads[n]:
                load.wait()
        diagonal = [-product(inverse(e), faces[0, e // 2, e % 2]) for e in range(4)]
        from_a, from_d = pick(diagonal[0], diagonal[1]), pick(diagonal[3], diagonal[2])
        put_block(sent, 0, from_a)
        put_block(sent, 1, from_d)
        put_block(sent, 2, pick(diagonal[1], diagonal[0]))
        put_block(sent, 3, pick(diagonal[2], diagonal[3]))
        for e in range(4):
            put_side(sent, e, e, diagonal[e])
        for load in loads[2]:
            load.wait()
        inv_b, inv_c = pick(inverse(1), inverse(0)), pick(inverse(2), inverse(3))
        gain_ba = product(inv_b, pick(span_face(1), span_face(0)))
        gain_bd = product(inv_b, pick(cross_face(1), cross_face(0)))
        gain_ca = product(inv_c, pick(cross_face(2), cross_face(3)))
        gain_cd = product(inv_c, pick(span_face(2), span_face(3)))
        for slot, source, gain, here, there in (
            (4, from_a, gain_ba, (1, 0), (0, 1)),
            (5, from_d, gain_bd, (1, 3), (0, 2)),
            (6, from_a, gain_ca, (2, 0), (3, 1)),
            (7, from_d, gain_cd, (2, 3), (3, 2)),
        ):
            block = -product(gain, source)
            nothing = jnp.zeros_like(block)
            put_block(sent, slot, block)
            put_side(sent, *here, pick(block, nothing))
            put_side(sent, *there, pick(nothing, block))
        sent[FLAG:] = jnp.where(even, 1.0, 0.0) + jnp.zeros((SENT - FLAG, 128), F32)
        for copy in to_site:
            pl.when(helper & ~goes_after)(copy.start)
        for copy in to_second:
            pl.when(~odd)(copy.start)
        spread(matrices.at[OWN], sent)
        matrices[OWN, ROWS:TWICE] = matrices[OWN, MAIN:ROWS]

    old_load.wait()
    rhs_load.wait()
    held = [old[e // 2, e % 2] for e in range(4)]
    old_b, old_c = pick(held[1], held[0]), pick(held[2], held[3])
    around_a = times_block(old_c, pick(cross_face(0), cross_face(1))) + times_block(
        old_b, pick(span_face(0), span_face(1))
    )
    around_d = times_block(old_b, pick(cross_face(3), cross_face(2))) + times_block(
        old_c, pick(span_face(3), span_face(2))
    )

    for load in loads[3]:
        load.wait()

    for _, receives, halo in halos:
        pl.when(receives)(halo.wait_recv)

    def part(e):
        j, k = e // 2, e % 2
        halo = jnp.where(*((has_left, halo_left[k]) if j == 0 else (has_right, halo_right[k])), 0.0)
        under = jnp.where(has_lower, below[j, k], 0.0)
        return (
            rhs[j, k]
            - times_block(under, faces[1, j, k])
            - times_block(halo, out_face(e))
        )

    for e in range(4):
        parts[e] = part(e)

    own_offset, first_offset = offsets.at[OWN], offsets.at[FIRST]
    offset_to_second = remote(own_offset, first_offset, (11, 23), at(1, 0))
    offset_to_site = remote(
        own_offset, offsets.at[2 + to_site_box], (12, 23 + to_site_box), at(to_site_step, 0)
    )

    @pl.when(flow == 1)
    def _():
        for load in loads[1]:
            load.wait()
        offset_to_second.wait_recv()
        for e in range(4):
            upper = jnp.concatenate(
                [
                    first_offset[:, 128 * e : 128 * e + 128],
                    first_offset[:, MAIN + 8 * e : MAIN + 8 * e + 7],
                ],
                axis=1,
            )
            parts[e] = parts[e] - times_block(upper, faces[0, e // 2, e % 2])

    total_a = pick(parts[0], parts[1]) - around_a
    total_d = pick(parts[3], parts[2]) - around_d

    @pl.when(~inner)
    def _():
        for load in loads[0]:
            load.wait()

    new_a = times_block(total_a, pick(inverse(0), inverse(1)))
    new_d = times_block(total_d, pick(inverse(3), inverse(2)))
    total_b = pick(parts[1], parts[0]) - (
        times_block(new_d, pick(cross_face(1), cross_face(0)))
        + times_block(new_a, pick(span_face(1), span_face(0)))
    )
    total_c = pick(parts[2], parts[3]) - (
        times_block(new_a, pick(cross_face(2), cross_face(3)))
        + times_block(new_d, pick(span_face(2), span_face(3)))
    )
    new_b = times_block(total_b, pick(inverse(1), inverse(0)))
    new_c = times_block(total_c, pick(inverse(2), inverse(3)))
    put_rows(own_offset, 0, pick(new_a, new_b))
    put_rows(own_offset, 1, pick(new_b, new_a))
    put_rows(own_offset, 2, pick(new_c, new_d))
    put_rows(own_offset, 3, pick(new_d, new_c))

    pl.when(~odd)(offset_to_second.start)
    pl.when(helper)(offset_to_site.start)

    @pl.when(signals)
    def _():
        for copy in to_site[:2]:
            copy.wait_send()
        pl.semaphore_signal(
            order_sem, inc=1, device_id=at(1 - 2 * core, 0), device_id_type=MESH
        )

    @pl.when(goes_after)
    def _():
        pl.semaphore_wait(order_sem, 1)
        for copy in to_site:
            copy.start()

    @pl.when(relays)
    def _():
        for arriving, onward in zip(to_relay, relay):
            arriving.wait_recv()
            onward.start()

    def state(slot, send_place, flow_step):
        return remote(leaving.at[slot], arrived.at[1], (send_place, 28), at(flow_step, 0))

    sends = [
        (flow == 27, state(1, 13, 4)),
        (among(23, 27), state(1, 14, 3)),
        (odd & ~among(11, 15, 17, 21, 25, 29, 31), state(1, 15, 2)),
        (odd & ~among(15, 21, 25, 29, 31), state(1, 16, 1)),
    ]
    express_sends = [
        (flow == 19, state(0, 17, 8)),
        (flow == 13, state(0, 18, 6)),
        (express, state(0, 19, 4)),
        (among(13, 19), state(0, 20, 3)),
    ]
    receives_state = sends[0][1].wait_recv

    def passed(box):
        first = 17 + 5 * box
        offset = offsets.at[2 + box]
        return in_parts(got.at[box], got.at[box], first, received(box), -1) + [
            remote(offset, offset, (first + PARTS, 23 + box), at(-1, 0))
        ]

    @pl.when(~inner)
    def _():
        leaving[1] = own_offset[...]
        for present, copy in sends:
            pl.when(present)(copy.start)

    @pl.when(inner)
    def _():
        base = jnp.where(odd, CHIP, OWN)
        own_used = jnp.where(flow == 13, MORE + 1, jnp.where(flow == 19, MORE + 2, CHIP))

        def compose(turn, carry):
            box = jnp.where((turn == 0) | (turn >= 3) | (flow == 9), turn, 3 - turn)
            layer = jnp.where(turn == 0, FIRST, 2 + box)
            held = jnp.where(turn == 0, OWN, jnp.where(turn == 1, base, MORE - 1 + turn))
            result = jnp.where(turn == 0, CHIP, MORE + turn)
            held_later = (
                (turn == 0) | before | ((flow == 13) & (turn == 1)) | ((flow == 19) & (turn <= 2))
            )
            later = jnp.where(held_later, held, layer)
            earlier = jnp.where(held_later, layer, held)

            @pl.when(express & (turn == more))
            def _():
                pack_turned(turned.at[1], matrices[own_used])

            for copy in in_parts(sent, got.at[box], 3, received(box), -1):
                copy.wait_recv()
            remote(own_offset, offsets.at[layer], (11, 23 + box), at(-1, 0)).wait_recv()

            @pl.when(passes & (turn > 0) & (turn < 3))
            def _():
                for copy in passed(box):
                    copy.start()

            spread(matrices.at[layer], got.at[box])
            matrices[result] = composed(weights, matrices[later], matrices[earlier])
            offsets[result] = step(offsets[earlier], weights[...]) + offsets[later]
            return carry

        lax.fori_loop(1 - core, 1 + more, compose, 0)

        used = jnp.where(more > 0, MORE + more, base)
        pack_turned(turned.at[0], matrices[used])

        turns = jnp.where(express, 3, 2)

        def advance(turn, carry):
            pl.when(turn == 1)(receives_state)
            last = turn == turns - 1
            own = express & last
            rows = arrived[jnp.where(turn == 0, 0, 1)]
            moved = fast_step(rows, turned.at[jnp.where(own, 1, 0)])
            leaving[jnp.where(last, 1, 0)] = moved + offsets[jnp.where(own, own_used, used)]

            @pl.when(express & (turn == 1))
            def _():
                for present, copy in express_sends:
                    pl.when(present)(copy.start)

            @pl.when(last)
            def _():
                for present, copy in sends:
                    pl.when(present)(copy.start)

            return carry

        lax.fori_loop(0, turns, advance, 0)

    rows = leaving[1]
    for e in range(4):
        out_ref[0, e // 2, e % 2, :, :128] = rows[:, 128 * e : 128 * e + 128]
        out_ref[0, e // 2, e % 2, :, 128:] = rows[:, MAIN + 8 * e : MAIN + 8 * e + 7]

    for present, copy in sends:
        pl.when(present)(copy.wait_send)

    for present, copy in express_sends:
        pl.when(present)(copy.wait_send)

    @pl.when(passes)
    def _():
        for box in (1, 2):
            for copy in passed(box):
                copy.wait_send()

    @pl.when(flow == 0)
    def _():
        for load in loads[1]:
            load.wait()

    for copy in to_second:
        pl.when(inner & ~odd)(copy.wait_send)
    pl.when(~odd)(offset_to_second.wait_send)
    for n, copy in enumerate(to_site):
        pl.when(helper & ~signals if n < 2 else helper)(copy.wait_send)
    for copy in relay:
        pl.when(relays)(copy.wait_send)
    pl.when(helper)(offset_to_site.wait_send)
    for sends, _, halo in halos:
        pl.when(sends)(halo.wait_send)


def body(flows, crosses, right_side, start_iterate, inverse_blocks, face_blocks, color_order):
    _, columns, spans, vectors, width = right_side.shape
    hbm = pl.BlockSpec(memory_space=pltpu.HBM)
    return pl.pallas_call(
        functools.partial(kernel, flows, crosses),
        out_shape=jax.ShapeDtypeStruct(right_side.shape, F32),
        in_specs=[hbm] * 5,
        out_specs=pl.BlockSpec(memory_space=pltpu.VMEM),
        scratch_shapes=[
            pltpu.SMEM((columns, spans), jnp.int32),
            pltpu.VMEM((columns, spans, vectors, width), F32),
            pltpu.VMEM((columns, spans, vectors, width), F32),
            pltpu.VMEM((columns, spans, width, width), F32),
            pltpu.VMEM((6, columns, spans, width, width), F32),
            pltpu.VMEM((spans, vectors, width), F32),
            pltpu.VMEM((spans, vectors, width), F32),
            pltpu.VMEM((columns, spans, vectors, width), F32),
            pltpu.VMEM((SENT, 128), F32),
            pltpu.VMEM((5, SENT, 128), F32),
            pltpu.VMEM((11, WIDE, WIDE), F32),
            pltpu.VMEM((11, vectors, WIDE), F32),
            pltpu.VMEM((2 * columns, vectors, width), F32),
            pltpu.VMEM((WIDE, DEEP), BF16),
            pltpu.VMEM((2, DEEP, WIDE), BF16),
            pltpu.VMEM((2, vectors, WIDE), F32),
            pltpu.VMEM((2, vectors, WIDE), F32),
            pltpu.SemaphoreType.DMA((27,)),
            pltpu.SemaphoreType.DMA((36,)),
            pltpu.SemaphoreType.DMA((33,)),
            pltpu.SemaphoreType.REGULAR,
        ],
        compiler_params=pltpu.CompilerParams(
            collective_id=0, has_side_effects=True, vmem_limit_bytes=(54 * 1024 - 128) * 1024
        ),
        cost_estimate=pl.CostEstimate(flops=10**9, bytes_accessed=4 * 10**6, transcendentals=0),
        name="sweep_chain",
    )(
        color_order,
        right_side,
        start_iterate,
        inverse_blocks.transpose(0, 1, 3, 2, 4),
        face_blocks.transpose(0, 1, 2, 4, 3, 5),
    )


def solution(mesh):
    return jax.shard_map(
        functools.partial(body, mesh.shape["flow"], mesh.shape["cross"]),
        mesh=mesh,
        in_specs=(
            P("flow", "cross", None, None, None),
            P("flow", "cross", None, None, None),
            P("flow", "cross", None, None, None),
            P("flow", None, "cross", None, None, None),
            P("flow", "cross", None),
        ),
        out_specs=P("flow", "cross", None, None, None),
        check_vma=False,
    )
```

```python
import functools

import jax
import jax.numpy as jnp
from jax import lax
from jax.experimental import pallas as pl
from jax.experimental.pallas import tpu as pltpu
from jax.sharding import PartitionSpec as P

MESH = pl.DeviceIdType.MESH
BF16 = jnp.bfloat16
F32 = jnp.float32
NN = (((1,), (0,)), ((), ()))
NT = (((1,), (1,)), ((), ()))

MAIN, REM, WIDE = 512, 32, 640
ROWS = MAIN + REM
TWICE = ROWS + REM
DEEP = 2 * MAIN + 128
EDGE, SIDE, FLAG, SENT = 1024, 1088, 1224, 1248
PARTS = 4
PART = SENT // PARTS
OWN, FIRST, CHIP, FAR, MORE = 0, 1, 2, 3, 5
PLACES = (
    ((0, 2), (None, 4), (None, 5), None),
    ((4, None), (2, 0), None, (5, None)),
    ((6, None), None, (3, 1), (7, None)),
    (None, (None, 6), (None, 7), (1, 3)),
)


def halves(value):
    high = value.astype(BF16)
    return high, (value - high.astype(F32)).astype(BF16)


def dot(a, b, dims):
    return lax.dot_general(a, b, dims, preferred_element_type=F32)


def product(a, b):
    a_high, a_low = halves(a)
    b_high, b_low = halves(b)
    return dot(a_high, b_high, NN) + dot(a_high, b_low, NN) + dot(a_low, b_high, NN)


def stacked(rows):
    high = rows.astype(BF16).astype(F32)
    return jnp.concatenate([high, rows - high], axis=0).astype(BF16)


def times_block(rows, block):
    both = stacked(rows)
    high, low = halves(block)
    out = dot(both, high, NT) + dot(both, low, NT)
    return out[:8] + out[8:]


def step(rows, weights):
    both = stacked(rows)
    main = both[:, :MAIN]
    out = (
        dot(main, weights[:, :MAIN], NT)
        + dot(main, weights[:, MAIN : 2 * MAIN], NT)
        + dot(both[:, MAIN:], weights[:, 2 * MAIN :], NT)
    )
    return out[:8] + out[8:]


def fast_step(rows, weights):
    both = stacked(rows)
    main = both[:, :MAIN]
    out = (
        dot(main, weights[:MAIN], NN)
        + dot(main, weights[MAIN : 2 * MAIN], NN)
        + dot(both[:, MAIN:], weights[2 * MAIN :], NN)
    )
    return out[:8] + out[8:]


def pack_turned(weights, matrix):
    high, low = halves(matrix.T)
    weights[:MAIN] = high[:MAIN]
    weights[MAIN : 2 * MAIN] = low[:MAIN]
    weights[2 * MAIN : 2 * MAIN + REM] = high[MAIN:ROWS]
    weights[2 * MAIN + REM : 2 * MAIN + 2 * REM] = low[MAIN:ROWS]
    weights[2 * MAIN + 2 * REM :] = jnp.zeros((128 - 2 * REM, WIDE), BF16)


def pack_weights(weights, matrix):
    high, low = halves(matrix)
    last = matrix[:, MAIN:]
    last_high = last.astype(BF16).astype(F32)
    tail = (
        last_high + pltpu.roll(last - last_high, REM, 1) + pltpu.roll(last_high, 2 * REM, 1)
    ).astype(BF16)
    for columns, values in (
        (slice(0, MAIN), high[:, :MAIN]),
        (slice(MAIN, 2 * MAIN), low[:, :MAIN]),
        (slice(2 * MAIN, DEEP), tail),
    ):
        weights[:ROWS, columns] = values[:ROWS]
        weights[ROWS:TWICE, columns] = values[MAIN:ROWS]
    weights[TWICE:, :] = jnp.zeros((WIDE - TWICE, DEEP), BF16)


def composed(weights, later, earlier):
    pack_weights(weights, later)
    high, low = halves(earlier)
    tail_high, tail_low = high[MAIN:ROWS], low[MAIN:ROWS]
    tail = jnp.concatenate([tail_high, tail_high, tail_low, jnp.zeros_like(tail_high)], axis=0)
    return (
        dot(weights[:, :MAIN], high[:MAIN], NN)
        + dot(weights[:, :MAIN], low[:MAIN], NN)
        + dot(weights[:, MAIN : 2 * MAIN], high[:MAIN], NN)
        + dot(weights[:, 2 * MAIN :], tail, NN)
    )


def put_block(sent, place, block):
    sent[128 * place : 128 * place + 128] = block[:128, :128]
    sent[EDGE + 8 * place : EDGE + 8 * place + 7] = block[128:, :128]


def put_side(sent, target, source, block):
    lane = 32 * target + 8 * source
    sent[SIDE : SIDE + 135, lane : lane + 7] = block[:, 128:]


def spread(matrix, sent):
    even = sent[FLAG : FLAG + 1] > 0.5
    lanes = lax.broadcasted_iota(jnp.int32, (1, 128), 1)

    def fetch(places, start, height):
        if places is None:
            return jnp.zeros((height, 128), F32)
        first, second = (
            0.0 if place is None else sent[start + height * place : start + height * place + height]
            for place in places
        )
        return jnp.where(even, first, second)

    side = sent[SIDE:FLAG]
    for target, row in enumerate(PLACES):
        top, edge = slice(128 * target, 128 * target + 128), slice(MAIN + 8 * target, MAIN + 8 * target + 8)
        for source, places in enumerate(row):
            columns = slice(128 * source, 128 * source + 128)
            matrix[top, columns] = fetch(places, 0, 128)
            matrix[edge, columns] = fetch(places, EDGE, 8)
        turned = side if target == 0 else pltpu.roll(side, 128 - 32 * target, 1)
        turned = jnp.where(lanes < REM, turned, 0.0)
        matrix[top, MAIN:] = turned[:128]
        matrix[edge, MAIN:] = turned[128:]


def put_rows(packed, element, rows):
    packed[:, 128 * element : 128 * element + 128] = rows[:, :128]
    packed[:, MAIN + 8 * element : MAIN + 8 * element + 7] = rows[:, 128:]
    packed[:, ROWS + 8 * element : ROWS + 8 * element + 7] = rows[:, 128:]


def kernel(
    flows,
    crosses,
    color_hbm,
    rhs_hbm,
    old_hbm,
    inv_hbm,
    faces_hbm,
    out_ref,
    colors,
    rhs,
    old,
    inv,
    faces,
    halo_left,
    halo_right,
    below,
    sent,
    got,
    matrices,
    offsets,
    parts,
    weights,
    turned,
    arrived,
    leaving,
    load_sem,
    send_sem,
    recv_sem,
    order_sem,
):
    flow, cross = lax.axis_index("flow"), lax.axis_index("cross")
    core = lax.rem(flow, 2)
    odd = core == 1
    has_left, has_right = cross > 0, cross < crosses - 1
    has_upper, has_lower = flow > 0, flow < flows - 1
    inner = flow > 1

    def among(*layers):
        return functools.reduce(jnp.logical_or, [flow == layer for layer in layers])

    before, express = among(19, 26, 27, 30, 31), among(9, 13, 21)
    more = jnp.where(
        flow == 9, 1, jnp.where(flow == 13, 3, jnp.where(among(19, 21, 26, 27, 30, 31), 2, 0))
    )
    passes = among(27, 31)
    helper = among(10, 11, 14, 15, 16, 17, 22, 23, 24, 25, 28, 29)
    signals, goes_after = among(22, 25, 29), among(23, 24, 28)
    to_site_step = jnp.where(
        among(10, 14, 22),
        -1,
        jnp.where(among(15, 23), -2, jnp.where(odd, 2, 3)),
    )
    relayed, relays = among(15, 16), among(4, 10)
    to_site_box = jnp.where(flow == 15, 3, 1 + core)

    def at(flow_step, cross_step):
        return (flow + flow_step, cross + cross_step)

    barrier = pltpu.get_barrier_semaphore()
    partners = [
        (has_upper, at(-1, 0)),
        (has_lower, at(1, 0)),
        (has_left, at(0, -1)),
        (has_right, at(0, 1)),
        (odd & (flow >= 2), at(-2, 0)),
        (odd & (flow < flows - 2), at(2, 0)),
    ]
    for distance, layers in (
        (3, (13, 16, 21, 24, 27, 28)),
        (4, (9, 13, 21, 27)),
        (5, (21,)),
        (6, (10, 13, 21)),
        (9, (4, 10)),
        (11, (4,)),
    ):
        partners.append((among(*layers), at(distance, 0)))
        partners.append((among(*(layer + distance for layer in layers)), at(-distance, 0)))

    def block_load(place, face, j, k):
        source = inv_hbm.at[0] if face is None else faces_hbm.at[0, face]
        target = inv if face is None else faces.at[face]
        return pltpu.make_async_copy(
            source.at[j, :, k, :], target.at[j, k], load_sem.at[place]
        )

    cells = [(j, k) for j in (0, 1) for k in (0, 1)]
    span_blocks = [(4, 0, 1), (4, 1, 1), (5, 0, 0), (5, 1, 0)]
    groups = [
        [(None, *cell) for cell in cells],
        [(0, *cell) for cell in cells],
        span_blocks + [(face, *cell) for face in (2, 3) for cell in cells],
        [(1, *cell) for cell in cells],
    ]
    count, loads = 0, []
    for group in groups:
        loads.append([block_load(count + n, *block) for n, block in enumerate(group)])
        count += len(group)
    old_load = pltpu.make_async_copy(old_hbm.at[0], old, load_sem.at[count])
    rhs_load = pltpu.make_async_copy(rhs_hbm.at[0], rhs, load_sem.at[count + 1])
    color_load = pltpu.make_async_copy(color_hbm.at[0], colors, load_sem.at[count + 2])
    color_load.start()
    old_load.start()
    rhs_load.start()

    @pl.when(inner)
    def _():
        for n in (0, 1, 2, 3):
            for load in loads[n]:
                load.start()

    @pl.when(~inner)
    def _():
        for n in (2, 3, 0, 1):
            for load in loads[n]:
                load.start()

    expected = 0
    for present, device in partners:
        expected = expected + present.astype(jnp.int32)

        @pl.when(present)
        def _(device=device):
            pl.semaphore_signal(barrier, inc=1, device_id=device, device_id_type=MESH)

    offsets[OWN] = jnp.zeros((8, WIDE), F32)
    arrived[0] = jnp.zeros((8, WIDE), F32)
    pl.semaphore_wait(barrier, expected)

    def remote(source, target, places, device):
        sending, receiving = places if isinstance(places, tuple) else (places, places)
        return pltpu.make_async_remote_copy(
            src_ref=source,
            dst_ref=target,
            send_sem=send_sem.at[sending],
            recv_sem=recv_sem.at[receiving],
            device_id=device,
            device_id_type=MESH,
        )

    halos = [
        (has_right, has_left, remote(old_hbm.at[0, 1], halo_left, 0, at(0, 1))),
        (has_left, has_right, remote(old_hbm.at[0, 0], halo_right, 1, at(0, -1))),
        (has_upper, has_lower, remote(old_hbm.at[0], below, 2, at(-1, 0))),
    ]
    for sends, _, halo in halos:
        pl.when(sends)(halo.start)

    color_load.wait()
    even = colors[0, 0] == 0

    def pick(first, second):
        return jnp.where(even, first, second)

    def cross_face(e):
        return faces[3 - e // 2, e // 2, e % 2]

    def span_face(e):
        return faces[5 - e % 2, e // 2, e % 2]

    def out_face(e):
        return faces[2 + e // 2, e // 2, e % 2]

    def inverse(e):
        return inv[e // 2, e % 2]

    def in_parts(source, target, sending, receiving, flow_step):
        return [
            remote(
                source.at[pl.ds(PART * n, PART)],
                target.at[pl.ds(PART * n, PART)],
                (sending + n, receiving + n),
                at(flow_step, 0),
            )
            for n in range(PARTS)
        ]

    def received(box):
        return 3 + PARTS * box

    to_second = in_parts(sent, got.at[0], 3, received(0), 1)
    to_site = in_parts(
        sent,
        got.at[jnp.where(relayed, 1, to_site_box)],
        7,
        jnp.where(relayed, 29, received(to_site_box)),
        jnp.where(flow == 15, -11, jnp.where(flow == 16, -6, to_site_step)),
    )
    relay_box = jnp.where(flow == 4, 3, 1)
    to_relay = in_parts(sent, got.at[1], 32, 29, -1)
    relay = in_parts(got.at[1], got.at[relay_box], 32, received(relay_box), 9)

    @pl.when(~inner)
    def _():
        for load in loads[2]:
            load.wait()

    @pl.when(inner)
    def _():
        sent[...] = jnp.zeros_like(sent)
        for slot in (OWN, FIRST, FAR, FAR + 1, FAR + 2):
            matrices[slot, ROWS:] = jnp.zeros((WIDE - ROWS, WIDE), F32)
        for n in (0, 1):
            for load in loads[n]:
                load.wait()
        diagonal = [-product(inverse(e), faces[0, e // 2, e % 2]) for e in range(4)]
        from_a, from_d = pick(diagonal[0], diagonal[1]), pick(diagonal[3], diagonal[2])
        put_block(sent, 0, from_a)
        put_block(sent, 1, from_d)
        put_block(sent, 2, pick(diagonal[1], diagonal[0]))
        put_block(sent, 3, pick(diagonal[2], diagonal[3]))
        for e in range(4):
            put_side(sent, e, e, diagonal[e])
        for load in loads[2]:
            load.wait()
        inv_b, inv_c = pick(inverse(1), inverse(0)), pick(inverse(2), inverse(3))
        gain_ba = product(inv_b, pick(span_face(1), span_face(0)))
        gain_bd = product(inv_b, pick(cross_face(1), cross_face(0)))
        gain_ca = product(inv_c, pick(cross_face(2), cross_face(3)))
        gain_cd = product(inv_c, pick(span_face(2), span_face(3)))
        for slot, source, gain, here, there in (
            (4, from_a, gain_ba, (1, 0), (0, 1)),
            (5, from_d, gain_bd, (1, 3), (0, 2)),
            (6, from_a, gain_ca, (2, 0), (3, 1)),
            (7, from_d, gain_cd, (2, 3), (3, 2)),
        ):
            block = -product(gain, source)
            nothing = jnp.zeros_like(block)
            put_block(sent, slot, block)
            put_side(sent, *here, pick(block, nothing))
            put_side(sent, *there, pick(nothing, block))
        sent[FLAG:] = jnp.where(even, 1.0, 0.0) + jnp.zeros((SENT - FLAG, 128), F32)
        for copy in to_site:
            pl.when(helper & ~goes_after)(copy.start)
        for copy in to_second:
            pl.when(~odd)(copy.start)
        spread(matrices.at[OWN], sent)
        matrices[OWN, ROWS:TWICE] = matrices[OWN, MAIN:ROWS]

    old_load.wait()
    rhs_load.wait()
    held = [old[e // 2, e % 2] for e in range(4)]
    old_b, old_c = pick(held[1], held[0]), pick(held[2], held[3])
    around_a = times_block(old_c, pick(cross_face(0), cross_face(1))) + times_block(
        old_b, pick(span_face(0), span_face(1))
    )
    around_d = times_block(old_b, pick(cross_face(3), cross_face(2))) + times_block(
        old_c, pick(span_face(3), span_face(2))
    )

    for load in loads[3]:
        load.wait()

    for _, receives, halo in halos:
        pl.when(receives)(halo.wait_recv)

    def part(e):
        j, k = e // 2, e % 2
        halo = jnp.where(*((has_left, halo_left[k]) if j == 0 else (has_right, halo_right[k])), 0.0)
        under = jnp.where(has_lower, below[j, k], 0.0)
        return (
            rhs[j, k]
            - times_block(under, faces[1, j, k])
            - times_block(halo, out_face(e))
        )

    for e in range(4):
        parts[e] = part(e)

    own_offset, first_offset = offsets.at[OWN], offsets.at[FIRST]
    offset_to_second = remote(own_offset, first_offset, (11, 23), at(1, 0))
    offset_to_site = remote(
        own_offset, offsets.at[2 + to_site_box], (12, 23 + to_site_box), at(to_site_step, 0)
    )

    @pl.when(flow == 1)
    def _():
        for load in loads[1]:
            load.wait()
        offset_to_second.wait_recv()
        for e in range(4):
            upper = jnp.concatenate(
                [
                    first_offset[:, 128 * e : 128 * e + 128],
                    first_offset[:, MAIN + 8 * e : MAIN + 8 * e + 7],
                ],
                axis=1,
            )
            parts[e] = parts[e] - times_block(upper, faces[0, e // 2, e % 2])

    total_a = pick(parts[0], parts[1]) - around_a
    total_d = pick(parts[3], parts[2]) - around_d

    @pl.when(~inner)
    def _():
        for load in loads[0]:
            load.wait()

    new_a = times_block(total_a, pick(inverse(0), inverse(1)))
    new_d = times_block(total_d, pick(inverse(3), inverse(2)))
    total_b = pick(parts[1], parts[0]) - (
        times_block(new_d, pick(cross_face(1), cross_face(0)))
        + times_block(new_a, pick(span_face(1), span_face(0)))
    )
    total_c = pick(parts[2], parts[3]) - (
        times_block(new_a, pick(cross_face(2), cross_face(3)))
        + times_block(new_d, pick(span_face(2), span_face(3)))
    )
    new_b = times_block(total_b, pick(inverse(1), inverse(0)))
    new_c = times_block(total_c, pick(inverse(2), inverse(3)))
    put_rows(own_offset, 0, pick(new_a, new_b))
    put_rows(own_offset, 1, pick(new_b, new_a))
    put_rows(own_offset, 2, pick(new_c, new_d))
    put_rows(own_offset, 3, pick(new_d, new_c))

    pl.when(~odd)(offset_to_second.start)
    pl.when(helper)(offset_to_site.start)

    @pl.when(signals)
    def _():
        for copy in to_site[:2]:
            copy.wait_send()
        pl.semaphore_signal(
            order_sem, inc=1, device_id=at(1 - 2 * core, 0), device_id_type=MESH
        )

    @pl.when(goes_after)
    def _():
        pl.semaphore_wait(order_sem, 1)
        for copy in to_site:
            copy.start()

    @pl.when(relays)
    def _():
        for arriving, onward in zip(to_relay, relay):
            arriving.wait_recv()
            onward.start()

    def state(slot, send_place, flow_step):
        return remote(leaving.at[slot], arrived.at[1], (send_place, 28), at(flow_step, 0))

    sends = [
        (flow == 27, state(1, 13, 4)),
        (flow == 27, state(1, 14, 3)),
        (odd & ~among(11, 15, 17, 23, 25, 29, 31), state(1, 15, 2)),
        (odd & ~among(15, 23, 25, 29, 31), state(1, 16, 1)),
    ]
    express_sends = [
        (among(13, 21), state(0, 17, 6)),
        (flow == 21, state(0, 18, 5)),
        (express, state(0, 19, 4)),
        (among(13, 21), state(0, 20, 3)),
    ]
    receives_state = sends[0][1].wait_recv

    def passed(box):
        first = 17 + 5 * box
        offset = offsets.at[2 + box]
        return in_parts(got.at[box], got.at[box], first, received(box), -1) + [
            remote(offset, offset, (first + PARTS, 23 + box), at(-1, 0))
        ]

    @pl.when(~inner)
    def _():
        leaving[1] = own_offset[...]
        for present, copy in sends:
            pl.when(present)(copy.start)

    @pl.when(inner)
    def _():
        base = jnp.where(odd, CHIP, OWN)
        own_used = jnp.where(flow == 13, MORE + 1, CHIP)

        def compose(turn, carry):
            box = jnp.where((turn == 0) | (turn == 3) | among(9, 21), turn, 3 - turn)
            layer = jnp.where(turn == 0, FIRST, 2 + box)
            held = jnp.where(turn == 0, OWN, jnp.where(turn == 1, base, MORE - 1 + turn))
            result = jnp.where(turn == 0, CHIP, MORE + turn)
            held_later = (turn == 0) | before | ((flow == 13) & (turn == 1))
            later = jnp.where(held_later, held, layer)
            earlier = jnp.where(held_later, layer, held)

            @pl.when(express & (turn == more))
            def _():
                pack_turned(turned.at[1], matrices[own_used])

            for copy in in_parts(sent, got.at[box], 3, received(box), -1):
                copy.wait_recv()
            remote(own_offset, offsets.at[layer], (11, 23 + box), at(-1, 0)).wait_recv()

            @pl.when(passes & (turn > 0))
            def _():
                for copy in passed(box):
                    copy.start()

            spread(matrices.at[layer], got.at[box])
            matrices[result] = composed(weights, matrices[later], matrices[earlier])
            offsets[result] = step(offsets[earlier], weights[...]) + offsets[later]
            return carry

        lax.fori_loop(1 - core, 1 + more, compose, 0)

        used = jnp.where(more > 0, MORE + more, base)
        pack_turned(turned.at[0], matrices[used])

        turns = jnp.where(express, 3, 2)

        def advance(turn, carry):
            pl.when(turn == 1)(receives_state)
            last = turn == turns - 1
            own = express & last
            rows = arrived[jnp.where(turn == 0, 0, 1)]
            moved = fast_step(rows, turned.at[jnp.where(own, 1, 0)])
            leaving[jnp.where(last, 1, 0)] = moved + offsets[jnp.where(own, own_used, used)]

            @pl.when(express & (turn == 1))
            def _():
                for present, copy in express_sends:
                    pl.when(present)(copy.start)

            @pl.when(last)
            def _():
                for present, copy in sends:
                    pl.when(present)(copy.start)

            return carry

        lax.fori_loop(0, turns, advance, 0)

    rows = leaving[1]
    for e in range(4):
        out_ref[0, e // 2, e % 2, :, :128] = rows[:, 128 * e : 128 * e + 128]
        out_ref[0, e // 2, e % 2, :, 128:] = rows[:, MAIN + 8 * e : MAIN + 8 * e + 7]

    for present, copy in sends:
        pl.when(present)(copy.wait_send)

    for present, copy in express_sends:
        pl.when(present)(copy.wait_send)

    @pl.when(passes)
    def _():
        for box in (1, 2):
            for copy in passed(box):
                copy.wait_send()

    @pl.when(flow == 0)
    def _():
        for load in loads[1]:
            load.wait()

    for copy in to_second:
        pl.when(inner & ~odd)(copy.wait_send)
    pl.when(~odd)(offset_to_second.wait_send)
    for n, copy in enumerate(to_site):
        pl.when(helper & ~signals if n < 2 else helper)(copy.wait_send)
    for copy in relay:
        pl.when(relays)(copy.wait_send)
    pl.when(helper)(offset_to_site.wait_send)
    for sends, _, halo in halos:
        pl.when(sends)(halo.wait_send)


def body(flows, crosses, right_side, start_iterate, inverse_blocks, face_blocks, color_order):
    _, columns, spans, vectors, width = right_side.shape
    hbm = pl.BlockSpec(memory_space=pltpu.HBM)
    return pl.pallas_call(
        functools.partial(kernel, flows, crosses),
        out_shape=jax.ShapeDtypeStruct(right_side.shape, F32),
        in_specs=[hbm] * 5,
        out_specs=pl.BlockSpec(memory_space=pltpu.VMEM),
        scratch_shapes=[
            pltpu.SMEM((columns, spans), jnp.int32),
            pltpu.VMEM((columns, spans, vectors, width), F32),
            pltpu.VMEM((columns, spans, vectors, width), F32),
            pltpu.VMEM((columns, spans, width, width), F32),
            pltpu.VMEM((6, columns, spans, width, width), F32),
            pltpu.VMEM((spans, vectors, width), F32),
            pltpu.VMEM((spans, vectors, width), F32),
            pltpu.VMEM((columns, spans, vectors, width), F32),
            pltpu.VMEM((SENT, 128), F32),
            pltpu.VMEM((4, SENT, 128), F32),
            pltpu.VMEM((9, WIDE, WIDE), F32),
            pltpu.VMEM((9, vectors, WIDE), F32),
            pltpu.VMEM((2 * columns, vectors, width), F32),
            pltpu.VMEM((WIDE, DEEP), BF16),
            pltpu.VMEM((2, DEEP, WIDE), BF16),
            pltpu.VMEM((2, vectors, WIDE), F32),
            pltpu.VMEM((2, vectors, WIDE), F32),
            pltpu.SemaphoreType.DMA((27,)),
            pltpu.SemaphoreType.DMA((36,)),
            pltpu.SemaphoreType.DMA((33,)),
            pltpu.SemaphoreType.REGULAR,
        ],
        compiler_params=pltpu.CompilerParams(
            collective_id=0, has_side_effects=True, vmem_limit_bytes=(54 * 1024 - 128) * 1024
        ),
        cost_estimate=pl.CostEstimate(flops=10**9, bytes_accessed=4 * 10**6, transcendentals=0),
        name="sweep_chain",
    )(
        color_order,
        right_side,
        start_iterate,
        inverse_blocks.transpose(0, 1, 3, 2, 4),
        face_blocks.transpose(0, 1, 2, 4, 3, 5),
    )


def solution(mesh):
    return jax.shard_map(
        functools.partial(body, mesh.shape["flow"], mesh.shape["cross"]),
        mesh=mesh,
        in_specs=(
            P("flow", "cross", None, None, None),
            P("flow", "cross", None, None, None),
            P("flow", "cross", None, None, None),
            P("flow", None, "cross", None, None, None),
            P("flow", "cross", None),
        ),
        out_specs=P("flow", "cross", None, None, None),
        check_vma=False,
    )
```

```python
import functools

import jax
import jax.numpy as jnp
from jax import lax
from jax.experimental import pallas as pl
from jax.experimental.pallas import tpu as pltpu
from jax.sharding import PartitionSpec as P

MESH = pl.DeviceIdType.MESH
BF16 = jnp.bfloat16
F32 = jnp.float32
NN = (((1,), (0,)), ((), ()))
NT = (((1,), (1,)), ((), ()))

MAIN, REM, WIDE = 512, 32, 640
ROWS = MAIN + REM
TWICE = ROWS + REM
DEEP = 2 * MAIN + 128
EDGE, SIDE, FLAG, SENT = 1024, 1088, 1224, 1248
PARTS = 4
PART = SENT // PARTS
OWN, FIRST, CHIP, FAR, MORE = 0, 1, 2, 3, 5
PLACES = (
    ((0, 2), (None, 4), (None, 5), None),
    ((4, None), (2, 0), None, (5, None)),
    ((6, None), None, (3, 1), (7, None)),
    (None, (None, 6), (None, 7), (1, 3)),
)


def halves(value):
    high = value.astype(BF16)
    return high, (value - high.astype(F32)).astype(BF16)


def dot(a, b, dims):
    return lax.dot_general(a, b, dims, preferred_element_type=F32)


def product(a, b):
    a_high, a_low = halves(a)
    b_high, b_low = halves(b)
    return dot(a_high, b_high, NN) + dot(a_high, b_low, NN) + dot(a_low, b_high, NN)


def stacked(rows):
    high = rows.astype(BF16).astype(F32)
    return jnp.concatenate([high, rows - high], axis=0).astype(BF16)


def times_block(rows, block):
    both = stacked(rows)
    high, low = halves(block)
    out = dot(both, high, NT) + dot(both, low, NT)
    return out[:8] + out[8:]


def step(rows, weights):
    both = stacked(rows)
    main = both[:, :MAIN]
    out = (
        dot(main, weights[:, :MAIN], NT)
        + dot(main, weights[:, MAIN : 2 * MAIN], NT)
        + dot(both[:, MAIN:], weights[:, 2 * MAIN :], NT)
    )
    return out[:8] + out[8:]


def fast_step(rows, weights):
    both = stacked(rows)
    main = both[:, :MAIN]
    out = (
        dot(main, weights[:MAIN], NN)
        + dot(main, weights[MAIN : 2 * MAIN], NN)
        + dot(both[:, MAIN:], weights[2 * MAIN :], NN)
    )
    return out[:8] + out[8:]


def pack_turned(weights, matrix):
    high, low = halves(matrix.T)
    weights[:MAIN] = high[:MAIN]
    weights[MAIN : 2 * MAIN] = low[:MAIN]
    weights[2 * MAIN : 2 * MAIN + REM] = high[MAIN:ROWS]
    weights[2 * MAIN + REM : 2 * MAIN + 2 * REM] = low[MAIN:ROWS]
    weights[2 * MAIN + 2 * REM :] = jnp.zeros((128 - 2 * REM, WIDE), BF16)


def pack_weights(weights, matrix):
    high, low = halves(matrix)
    last = matrix[:, MAIN:]
    last_high = last.astype(BF16).astype(F32)
    tail = (
        last_high + pltpu.roll(last - last_high, REM, 1) + pltpu.roll(last_high, 2 * REM, 1)
    ).astype(BF16)
    for columns, values in (
        (slice(0, MAIN), high[:, :MAIN]),
        (slice(MAIN, 2 * MAIN), low[:, :MAIN]),
        (slice(2 * MAIN, DEEP), tail),
    ):
        weights[:ROWS, columns] = values[:ROWS]
        weights[ROWS:TWICE, columns] = values[MAIN:ROWS]
    weights[TWICE:, :] = jnp.zeros((WIDE - TWICE, DEEP), BF16)


def composed(weights, later, earlier):
    pack_weights(weights, later)
    high, low = halves(earlier)
    tail_high, tail_low = high[MAIN:ROWS], low[MAIN:ROWS]
    tail = jnp.concatenate([tail_high, tail_high, tail_low, jnp.zeros_like(tail_high)], axis=0)
    return (
        dot(weights[:, :MAIN], high[:MAIN], NN)
        + dot(weights[:, :MAIN], low[:MAIN], NN)
        + dot(weights[:, MAIN : 2 * MAIN], high[:MAIN], NN)
        + dot(weights[:, 2 * MAIN :], tail, NN)
    )


def put_block(sent, place, block):
    sent[128 * place : 128 * place + 128] = block[:128, :128]
    sent[EDGE + 8 * place : EDGE + 8 * place + 7] = block[128:, :128]


def put_side(sent, target, source, block):
    lane = 32 * target + 8 * source
    sent[SIDE : SIDE + 135, lane : lane + 7] = block[:, 128:]


def spread(matrix, sent):
    even = sent[FLAG : FLAG + 1] > 0.5
    lanes = lax.broadcasted_iota(jnp.int32, (1, 128), 1)

    def fetch(places, start, height):
        if places is None:
            return jnp.zeros((height, 128), F32)
        first, second = (
            0.0 if place is None else sent[start + height * place : start + height * place + height]
            for place in places
        )
        return jnp.where(even, first, second)

    side = sent[SIDE:FLAG]
    for target, row in enumerate(PLACES):
        top, edge = slice(128 * target, 128 * target + 128), slice(MAIN + 8 * target, MAIN + 8 * target + 8)
        for source, places in enumerate(row):
            columns = slice(128 * source, 128 * source + 128)
            matrix[top, columns] = fetch(places, 0, 128)
            matrix[edge, columns] = fetch(places, EDGE, 8)
        turned = side if target == 0 else pltpu.roll(side, 128 - 32 * target, 1)
        turned = jnp.where(lanes < REM, turned, 0.0)
        matrix[top, MAIN:] = turned[:128]
        matrix[edge, MAIN:] = turned[128:]


def put_rows(packed, element, rows):
    packed[:, 128 * element : 128 * element + 128] = rows[:, :128]
    packed[:, MAIN + 8 * element : MAIN + 8 * element + 7] = rows[:, 128:]
    packed[:, ROWS + 8 * element : ROWS + 8 * element + 7] = rows[:, 128:]


def kernel(
    flows,
    crosses,
    color_hbm,
    rhs_hbm,
    old_hbm,
    inv_hbm,
    faces_hbm,
    out_ref,
    colors,
    rhs,
    old,
    inv,
    faces,
    halo_left,
    halo_right,
    below,
    sent,
    got,
    matrices,
    offsets,
    parts,
    weights,
    turned,
    arrived,
    leaving,
    load_sem,
    send_sem,
    recv_sem,
    order_sem,
    ready_right,
    ready_later,
):
    flow, cross = lax.axis_index("flow"), lax.axis_index("cross")
    core = lax.rem(flow, 2)
    odd = core == 1
    has_left, has_right = cross > 0, cross < crosses - 1
    has_upper, has_lower = flow > 0, flow < flows - 1
    inner = flow > 1

    def among(*layers):
        return functools.reduce(jnp.logical_or, [flow == layer for layer in layers])

    before, express = among(19, 26, 27, 30, 31), among(9, 13, 21)
    more = jnp.where(
        flow == 9, 1, jnp.where(flow == 13, 3, jnp.where(among(19, 21, 26, 27, 30, 31), 2, 0))
    )
    passes = among(27, 31)
    helper = among(10, 11, 14, 15, 16, 17, 22, 23, 24, 25, 28, 29)
    signals, goes_after = among(22, 25, 29), among(23, 24, 28)
    to_site_step = jnp.where(
        among(10, 14, 22),
        -1,
        jnp.where(among(15, 23), -2, jnp.where(odd, 2, 3)),
    )
    relayed, relays = among(15, 16), among(4, 10)
    to_site_box = jnp.where(flow == 15, 3, 1 + core)

    def at(flow_step, cross_step):
        return (flow + flow_step, cross + cross_step)

    barrier = pltpu.get_barrier_semaphore()
    earlier_ones = [(has_upper, at(-1, 0)), (odd & (flow >= 2), at(-2, 0))]
    later_ones = [(has_lower, at(1, 0)), (odd & (flow < flows - 2), at(2, 0))]
    for distance, layers in (
        (3, (13, 16, 21, 24, 27, 28)),
        (4, (9, 13, 21, 27)),
        (5, (21,)),
        (6, (10, 13, 21)),
        (9, (4, 10)),
        (11, (4,)),
    ):
        later_ones.append((among(*layers), at(distance, 0)))
        earlier_ones.append((among(*(layer + distance for layer in layers)), at(-distance, 0)))

    def block_load(place, face, j, k):
        source = inv_hbm.at[0] if face is None else faces_hbm.at[0, face]
        target = inv if face is None else faces.at[face]
        return pltpu.make_async_copy(
            source.at[j, :, k, :], target.at[j, k], load_sem.at[place]
        )

    cells = [(j, k) for j in (0, 1) for k in (0, 1)]
    span_blocks = [(4, 0, 1), (4, 1, 1), (5, 0, 0), (5, 1, 0)]
    groups = [
        [(None, *cell) for cell in cells],
        [(0, *cell) for cell in cells],
        span_blocks + [(face, *cell) for face in (2, 3) for cell in cells],
        [(1, *cell) for cell in cells],
    ]
    count, loads = 0, []
    for group in groups:
        loads.append([block_load(count + n, *block) for n, block in enumerate(group)])
        count += len(group)
    old_load = pltpu.make_async_copy(old_hbm.at[0], old, load_sem.at[count])
    rhs_load = pltpu.make_async_copy(rhs_hbm.at[0], rhs, load_sem.at[count + 1])
    color_load = pltpu.make_async_copy(color_hbm.at[0], colors, load_sem.at[count + 2])
    color_load.start()
    old_load.start()
    rhs_load.start()

    @pl.when(inner)
    def _():
        for n in (0, 1, 2, 3):
            for load in loads[n]:
                load.start()

    @pl.when(~inner)
    def _():
        for n in (2, 3, 0, 1):
            for load in loads[n]:
                load.start()

    def counted(devices):
        return sum(present.astype(jnp.int32) for present, _ in devices)

    def tell(semaphore, devices):
        for present, device in devices:

            @pl.when(present)
            def _(device=device):
                pl.semaphore_signal(
                    semaphore, inc=1, device_id=device, device_id_type=MESH
                )

    tell(barrier, [(has_right, at(0, 1))] + later_ones)

    offsets[OWN] = jnp.zeros((8, WIDE), F32)
    @pl.when(has_left | has_upper)
    def _():
        pl.semaphore_wait(barrier, has_left.astype(jnp.int32) + counted(earlier_ones))

    tell(ready_right, [(has_left, at(0, -1))])

    def remote(source, target, places, device):
        sending, receiving = places if isinstance(places, tuple) else (places, places)
        return pltpu.make_async_remote_copy(
            src_ref=source,
            dst_ref=target,
            send_sem=send_sem.at[sending],
            recv_sem=recv_sem.at[receiving],
            device_id=device,
            device_id_type=MESH,
        )

    halos = [
        (has_right, has_left, remote(old_hbm.at[0, 1], halo_left, 0, at(0, 1))),
        (has_left, has_right, remote(old_hbm.at[0, 0], halo_right, 1, at(0, -1))),
        (has_upper, has_lower, remote(old_hbm.at[0], below, 2, at(-1, 0))),
    ]
    for sends, _, halo in halos[1:]:
        pl.when(sends)(halo.start)
    tell(ready_later, earlier_ones)

    @pl.when(has_right)
    def _():
        pl.semaphore_wait(ready_right, 1)
        halos[0][2].start()

    color_load.wait()
    even = colors[0, 0] == 0

    def pick(first, second):
        return jnp.where(even, first, second)

    def cross_face(e):
        return faces[3 - e // 2, e // 2, e % 2]

    def span_face(e):
        return faces[5 - e % 2, e // 2, e % 2]

    def out_face(e):
        return faces[2 + e // 2, e // 2, e % 2]

    def inverse(e):
        return inv[e // 2, e % 2]

    def in_parts(source, target, sending, receiving, flow_step):
        return [
            remote(
                source.at[pl.ds(PART * n, PART)],
                target.at[pl.ds(PART * n, PART)],
                (sending + n, receiving + n),
                at(flow_step, 0),
            )
            for n in range(PARTS)
        ]

    def received(box):
        return 3 + PARTS * box

    to_second = in_parts(sent, got.at[0], 3, received(0), 1)
    to_site = in_parts(
        sent,
        got.at[jnp.where(relayed, 1, to_site_box)],
        7,
        jnp.where(relayed, 29, received(to_site_box)),
        jnp.where(flow == 15, -11, jnp.where(flow == 16, -6, to_site_step)),
    )
    relay_box = jnp.where(flow == 4, 3, 1)
    to_relay = in_parts(sent, got.at[1], 32, 29, -1)
    relay = in_parts(got.at[1], got.at[relay_box], 32, received(relay_box), 9)

    @pl.when(~inner)
    def _():
        for load in loads[2]:
            load.wait()

    @pl.when(inner)
    def _():
        sent[...] = jnp.zeros_like(sent)
        for slot in (OWN, FIRST, FAR, FAR + 1, FAR + 2):
            matrices[slot, ROWS:] = jnp.zeros((WIDE - ROWS, WIDE), F32)
        for n in (0, 1):
            for load in loads[n]:
                load.wait()
        diagonal = [-product(inverse(e), faces[0, e // 2, e % 2]) for e in range(4)]
        from_a, from_d = pick(diagonal[0], diagonal[1]), pick(diagonal[3], diagonal[2])
        put_block(sent, 0, from_a)
        put_block(sent, 1, from_d)
        put_block(sent, 2, pick(diagonal[1], diagonal[0]))
        put_block(sent, 3, pick(diagonal[2], diagonal[3]))
        for e in range(4):
            put_side(sent, e, e, diagonal[e])
        for load in loads[2]:
            load.wait()
        inv_b, inv_c = pick(inverse(1), inverse(0)), pick(inverse(2), inverse(3))
        gain_ba = product(inv_b, pick(span_face(1), span_face(0)))
        gain_bd = product(inv_b, pick(cross_face(1), cross_face(0)))
        gain_ca = product(inv_c, pick(cross_face(2), cross_face(3)))
        gain_cd = product(inv_c, pick(span_face(2), span_face(3)))
        for slot, source, gain, here, there in (
            (4, from_a, gain_ba, (1, 0), (0, 1)),
            (5, from_d, gain_bd, (1, 3), (0, 2)),
            (6, from_a, gain_ca, (2, 0), (3, 1)),
            (7, from_d, gain_cd, (2, 3), (3, 2)),
        ):
            block = -product(gain, source)
            nothing = jnp.zeros_like(block)
            put_block(sent, slot, block)
            put_side(sent, *here, pick(block, nothing))
            put_side(sent, *there, pick(nothing, block))
        sent[FLAG:] = jnp.where(even, 1.0, 0.0) + jnp.zeros((SENT - FLAG, 128), F32)
        @pl.when(has_lower)
        def _():
            pl.semaphore_wait(ready_later, counted(later_ones))

        for copy in to_site:
            pl.when(helper & ~goes_after)(copy.start)
        for copy in to_second:
            pl.when(~odd)(copy.start)
        spread(matrices.at[OWN], sent)
        matrices[OWN, ROWS:TWICE] = matrices[OWN, MAIN:ROWS]

    old_load.wait()
    rhs_load.wait()
    held = [old[e // 2, e % 2] for e in range(4)]
    old_b, old_c = pick(held[1], held[0]), pick(held[2], held[3])
    around_a = times_block(old_c, pick(cross_face(0), cross_face(1))) + times_block(
        old_b, pick(span_face(0), span_face(1))
    )
    around_d = times_block(old_b, pick(cross_face(3), cross_face(2))) + times_block(
        old_c, pick(span_face(3), span_face(2))
    )

    for load in loads[3]:
        load.wait()

    for _, receives, halo in halos:
        pl.when(receives)(halo.wait_recv)

    def part(e):
        j, k = e // 2, e % 2
        halo = jnp.where(*((has_left, halo_left[k]) if j == 0 else (has_right, halo_right[k])), 0.0)
        under = jnp.where(has_lower, below[j, k], 0.0)
        return (
            rhs[j, k]
            - times_block(under, faces[1, j, k])
            - times_block(halo, out_face(e))
        )

    for e in range(4):
        parts[e] = part(e)

    own_offset, first_offset = offsets.at[OWN], offsets.at[FIRST]
    offset_to_second = remote(own_offset, first_offset, (11, 23), at(1, 0))
    offset_to_site = remote(
        own_offset, offsets.at[2 + to_site_box], (12, 23 + to_site_box), at(to_site_step, 0)
    )

    @pl.when(flow == 1)
    def _():
        for load in loads[1]:
            load.wait()
        offset_to_second.wait_recv()
        for e in range(4):
            upper = jnp.concatenate(
                [
                    first_offset[:, 128 * e : 128 * e + 128],
                    first_offset[:, MAIN + 8 * e : MAIN + 8 * e + 7],
                ],
                axis=1,
            )
            parts[e] = parts[e] - times_block(upper, faces[0, e // 2, e % 2])

    total_a = pick(parts[0], parts[1]) - around_a
    total_d = pick(parts[3], parts[2]) - around_d

    @pl.when(~inner)
    def _():
        for load in loads[0]:
            load.wait()

    new_a = times_block(total_a, pick(inverse(0), inverse(1)))
    new_d = times_block(total_d, pick(inverse(3), inverse(2)))
    total_b = pick(parts[1], parts[0]) - (
        times_block(new_d, pick(cross_face(1), cross_face(0)))
        + times_block(new_a, pick(span_face(1), span_face(0)))
    )
    total_c = pick(parts[2], parts[3]) - (
        times_block(new_a, pick(cross_face(2), cross_face(3)))
        + times_block(new_d, pick(span_face(2), span_face(3)))
    )
    new_b = times_block(total_b, pick(inverse(1), inverse(0)))
    new_c = times_block(total_c, pick(inverse(2), inverse(3)))
    put_rows(own_offset, 0, pick(new_a, new_b))
    put_rows(own_offset, 1, pick(new_b, new_a))
    put_rows(own_offset, 2, pick(new_c, new_d))
    put_rows(own_offset, 3, pick(new_d, new_c))

    @pl.when(~inner)
    def _():
        pl.semaphore_wait(ready_later, counted(later_ones))

    pl.when(~odd)(offset_to_second.start)
    pl.when(helper)(offset_to_site.start)

    @pl.when(signals)
    def _():
        for copy in to_site[:2]:
            copy.wait_send()
        pl.semaphore_signal(
            order_sem, inc=1, device_id=at(1 - 2 * core, 0), device_id_type=MESH
        )

    @pl.when(goes_after)
    def _():
        pl.semaphore_wait(order_sem, 1)
        for copy in to_site:
            copy.start()

    @pl.when(relays)
    def _():
        for arriving, onward in zip(to_relay, relay):
            arriving.wait_recv()
            onward.start()

    def state(slot, send_place, flow_step):
        return remote(leaving.at[slot], arrived, (send_place, 28), at(flow_step, 0))

    sends = [
        (flow == 27, state(1, 13, 4)),
        (flow == 27, state(1, 14, 3)),
        (odd & ~among(11, 15, 17, 23, 25, 29, 31), state(1, 15, 2)),
        (odd & ~among(15, 23, 25, 29, 31), state(1, 16, 1)),
    ]
    express_sends = [
        (among(13, 21), state(0, 17, 6)),
        (flow == 21, state(0, 18, 5)),
        (express, state(0, 19, 4)),
        (among(13, 21), state(0, 20, 3)),
    ]
    receives_state = sends[0][1].wait_recv

    def passed(box):
        first = 17 + 5 * box
        offset = offsets.at[2 + box]
        return in_parts(got.at[box], got.at[box], first, received(box), -1) + [
            remote(offset, offset, (first + PARTS, 23 + box), at(-1, 0))
        ]

    @pl.when(~inner)
    def _():
        leaving[1] = own_offset[...]
        for present, copy in sends:
            pl.when(present)(copy.start)

    @pl.when(inner)
    def _():
        base = jnp.where(odd, CHIP, OWN)
        own_used = jnp.where(flow == 13, MORE + 1, CHIP)

        def compose(turn, carry):
            box = jnp.where((turn == 0) | (turn == 3) | among(9, 21), turn, 3 - turn)
            layer = jnp.where(turn == 0, FIRST, 2 + box)
            held = jnp.where(turn == 0, OWN, jnp.where(turn == 1, base, MORE - 1 + turn))
            result = jnp.where(turn == 0, CHIP, MORE + turn)
            held_later = (turn == 0) | before | ((flow == 13) & (turn == 1))
            later = jnp.where(held_later, held, layer)
            earlier = jnp.where(held_later, layer, held)

            @pl.when(express & (turn == more))
            def _():
                pack_turned(turned.at[1], matrices[own_used])

            for copy in in_parts(sent, got.at[box], 3, received(box), -1):
                copy.wait_recv()
            remote(own_offset, offsets.at[layer], (11, 23 + box), at(-1, 0)).wait_recv()

            @pl.when(passes & (turn > 0))
            def _():
                for copy in passed(box):
                    copy.start()

            spread(matrices.at[layer], got.at[box])
            matrices[result] = composed(weights, matrices[later], matrices[earlier])
            offsets[result] = step(offsets[earlier], weights[...]) + offsets[later]
            return carry

        lax.fori_loop(1 - core, 1 + more, compose, 0)

        used = jnp.where(more > 0, MORE + more, base)
        pack_turned(turned.at[0], matrices[used])

        turns = jnp.where(express, 3, 2)

        def advance(turn, carry):
            pl.when(turn == 1)(receives_state)
            last = turn == turns - 1
            own = express & last
            rows = arrived[...]
            moved = fast_step(rows, turned.at[jnp.where(own, 1, 0)])
            leaving[jnp.where(last, 1, 0)] = moved + offsets[jnp.where(own, own_used, used)]

            @pl.when(express & (turn == 1))
            def _():
                for present, copy in express_sends:
                    pl.when(present)(copy.start)

            @pl.when(last)
            def _():
                for present, copy in sends:
                    pl.when(present)(copy.start)

            return carry

        lax.fori_loop(1, turns, advance, 0)

    rows = leaving[1]
    for e in range(4):
        out_ref[0, e // 2, e % 2, :, :128] = rows[:, 128 * e : 128 * e + 128]
        out_ref[0, e // 2, e % 2, :, 128:] = rows[:, MAIN + 8 * e : MAIN + 8 * e + 7]

    for present, copy in sends:
        pl.when(present)(copy.wait_send)

    for present, copy in express_sends:
        pl.when(present)(copy.wait_send)

    @pl.when(passes)
    def _():
        for box in (1, 2):
            for copy in passed(box):
                copy.wait_send()

    @pl.when(flow == 0)
    def _():
        for load in loads[1]:
            load.wait()

    for copy in to_second:
        pl.when(inner & ~odd)(copy.wait_send)
    pl.when(~odd)(offset_to_second.wait_send)
    for n, copy in enumerate(to_site):
        pl.when(helper & ~signals if n < 2 else helper)(copy.wait_send)
    for copy in relay:
        pl.when(relays)(copy.wait_send)
    pl.when(helper)(offset_to_site.wait_send)
    for sends, _, halo in halos:
        pl.when(sends)(halo.wait_send)


def body(flows, crosses, right_side, start_iterate, inverse_blocks, face_blocks, color_order):
    _, columns, spans, vectors, width = right_side.shape
    hbm = pl.BlockSpec(memory_space=pltpu.HBM)
    return pl.pallas_call(
        functools.partial(kernel, flows, crosses),
        out_shape=jax.ShapeDtypeStruct(right_side.shape, F32),
        in_specs=[hbm] * 5,
        out_specs=pl.BlockSpec(memory_space=pltpu.VMEM),
        scratch_shapes=[
            pltpu.SMEM((columns, spans), jnp.int32),
            pltpu.VMEM((columns, spans, vectors, width), F32),
            pltpu.VMEM((columns, spans, vectors, width), F32),
            pltpu.VMEM((columns, spans, width, width), F32),
            pltpu.VMEM((6, columns, spans, width, width), F32),
            pltpu.VMEM((spans, vectors, width), F32),
            pltpu.VMEM((spans, vectors, width), F32),
            pltpu.VMEM((columns, spans, vectors, width), F32),
            pltpu.VMEM((SENT, 128), F32),
            pltpu.VMEM((4, SENT, 128), F32),
            pltpu.VMEM((9, WIDE, WIDE), F32),
            pltpu.VMEM((9, vectors, WIDE), F32),
            pltpu.VMEM((2 * columns, vectors, width), F32),
            pltpu.VMEM((WIDE, DEEP), BF16),
            pltpu.VMEM((2, DEEP, WIDE), BF16),
            pltpu.VMEM((vectors, WIDE), F32),
            pltpu.VMEM((2, vectors, WIDE), F32),
            pltpu.SemaphoreType.DMA((27,)),
            pltpu.SemaphoreType.DMA((36,)),
            pltpu.SemaphoreType.DMA((33,)),
            pltpu.SemaphoreType.REGULAR,
            pltpu.SemaphoreType.REGULAR,
            pltpu.SemaphoreType.REGULAR,
        ],
        compiler_params=pltpu.CompilerParams(
            collective_id=0, has_side_effects=True, vmem_limit_bytes=(54 * 1024 - 128) * 1024
        ),
        cost_estimate=pl.CostEstimate(flops=10**9, bytes_accessed=4 * 10**6, transcendentals=0),
        name="sweep_chain",
    )(
        color_order,
        right_side,
        start_iterate,
        inverse_blocks.transpose(0, 1, 3, 2, 4),
        face_blocks.transpose(0, 1, 2, 4, 3, 5),
    )


def solution(mesh):
    return jax.shard_map(
        functools.partial(body, mesh.shape["flow"], mesh.shape["cross"]),
        mesh=mesh,
        in_specs=(
            P("flow", "cross", None, None, None),
            P("flow", "cross", None, None, None),
            P("flow", "cross", None, None, None),
            P("flow", None, "cross", None, None, None),
            P("flow", "cross", None),
        ),
        out_specs=P("flow", "cross", None, None, None),
        check_vma=False,
    )
```

```python
import functools

import jax
import jax.numpy as jnp
from jax import lax
from jax.experimental import pallas as pl
from jax.experimental.pallas import tpu as pltpu
from jax.sharding import PartitionSpec as P

MESH = pl.DeviceIdType.MESH
BF16 = jnp.bfloat16
F32 = jnp.float32
NN = (((1,), (0,)), ((), ()))
NT = (((1,), (1,)), ((), ()))

MAIN, REM, WIDE = 512, 32, 640
ROWS = MAIN + REM
TWICE = ROWS + REM
DEEP = 2 * MAIN + 128
EDGE, SIDE, FLAG, SENT = 1024, 1088, 1224, 1248
PARTS = 4
PART = SENT // PARTS
OWN, FIRST, CHIP, FAR, MORE = 0, 1, 2, 3, 5
PLACES = (
    ((0, 2), (None, 4), (None, 5), None),
    ((4, None), (2, 0), None, (5, None)),
    ((6, None), None, (3, 1), (7, None)),
    (None, (None, 6), (None, 7), (1, 3)),
)


def halves(value):
    high = value.astype(BF16)
    return high, (value - high.astype(F32)).astype(BF16)


def dot(a, b, dims):
    return lax.dot_general(a, b, dims, preferred_element_type=F32)


def product(a, b):
    a_high, a_low = halves(a)
    b_high, b_low = halves(b)
    return dot(a_high, b_high, NN) + dot(a_high, b_low, NN) + dot(a_low, b_high, NN)


def stacked(rows):
    high = rows.astype(BF16).astype(F32)
    return jnp.concatenate([high, rows - high], axis=0).astype(BF16)


def times_block(rows, block):
    both = stacked(rows)
    high, low = halves(block)
    out = dot(both, high, NT) + dot(both, low, NT)
    return out[:8] + out[8:]


def step(rows, weights):
    both = stacked(rows)
    main = both[:, :MAIN]
    out = (
        dot(main, weights[:, :MAIN], NT)
        + dot(main, weights[:, MAIN : 2 * MAIN], NT)
        + dot(both[:, MAIN:], weights[:, 2 * MAIN :], NT)
    )
    return out[:8] + out[8:]


def fast_step(rows, weights):
    both = stacked(rows)
    main = both[:, :MAIN]
    out = (
        dot(main, weights[:MAIN], NN)
        + dot(main, weights[MAIN : 2 * MAIN], NN)
        + dot(both[:, MAIN:], weights[2 * MAIN :], NN)
    )
    return out[:8] + out[8:]


def pack_turned(weights, matrix):
    high, low = halves(matrix.T)
    weights[:MAIN] = high[:MAIN]
    weights[MAIN : 2 * MAIN] = low[:MAIN]
    weights[2 * MAIN : 2 * MAIN + REM] = high[MAIN:ROWS]
    weights[2 * MAIN + REM : 2 * MAIN + 2 * REM] = low[MAIN:ROWS]
    weights[2 * MAIN + 2 * REM :] = jnp.zeros((128 - 2 * REM, WIDE), BF16)


def pack_weights(weights, matrix):
    high, low = halves(matrix)
    last = matrix[:, MAIN:]
    last_high = last.astype(BF16).astype(F32)
    tail = (
        last_high + pltpu.roll(last - last_high, REM, 1) + pltpu.roll(last_high, 2 * REM, 1)
    ).astype(BF16)
    for columns, values in (
        (slice(0, MAIN), high[:, :MAIN]),
        (slice(MAIN, 2 * MAIN), low[:, :MAIN]),
        (slice(2 * MAIN, DEEP), tail),
    ):
        weights[:ROWS, columns] = values[:ROWS]
        weights[ROWS:TWICE, columns] = values[MAIN:ROWS]
    weights[TWICE:, :] = jnp.zeros((WIDE - TWICE, DEEP), BF16)


def composed(weights, later, earlier):
    pack_weights(weights, later)
    high, low = halves(earlier)
    tail_high, tail_low = high[MAIN:ROWS], low[MAIN:ROWS]
    tail = jnp.concatenate([tail_high, tail_high, tail_low, jnp.zeros_like(tail_high)], axis=0)
    return (
        dot(weights[:TWICE, :MAIN], high[:MAIN], NN)
        + dot(weights[:TWICE, :MAIN], low[:MAIN], NN)
        + dot(weights[:TWICE, MAIN : 2 * MAIN], high[:MAIN], NN)
        + dot(weights[:TWICE, 2 * MAIN :], tail, NN)
    )


def put_block(sent, place, block):
    sent[128 * place : 128 * place + 128] = block[:128, :128]
    sent[EDGE + 8 * place : EDGE + 8 * place + 7] = block[128:, :128]


def put_side(sent, target, source, block):
    lane = 32 * target + 8 * source
    sent[SIDE : SIDE + 135, lane : lane + 7] = block[:, 128:]


def spread(matrix, sent):
    even = sent[FLAG : FLAG + 1] > 0.5
    lanes = lax.broadcasted_iota(jnp.int32, (1, 128), 1)

    def fetch(places, start, height):
        if places is None:
            return jnp.zeros((height, 128), F32)
        first, second = (
            0.0 if place is None else sent[start + height * place : start + height * place + height]
            for place in places
        )
        return jnp.where(even, first, second)

    side = sent[SIDE:FLAG]
    for target, row in enumerate(PLACES):
        top, edge = slice(128 * target, 128 * target + 128), slice(MAIN + 8 * target, MAIN + 8 * target + 8)
        for source, places in enumerate(row):
            columns = slice(128 * source, 128 * source + 128)
            matrix[top, columns] = fetch(places, 0, 128)
            matrix[edge, columns] = fetch(places, EDGE, 8)
        turned = side if target == 0 else pltpu.roll(side, 128 - 32 * target, 1)
        turned = jnp.where(lanes < REM, turned, 0.0)
        matrix[top, MAIN:] = turned[:128]
        matrix[edge, MAIN:] = turned[128:]


def put_rows(packed, element, rows):
    packed[:, 128 * element : 128 * element + 128] = rows[:, :128]
    packed[:, MAIN + 8 * element : MAIN + 8 * element + 7] = rows[:, 128:]
    packed[:, ROWS + 8 * element : ROWS + 8 * element + 7] = rows[:, 128:]


def kernel(
    flows,
    crosses,
    color_hbm,
    rhs_hbm,
    old_hbm,
    inv_hbm,
    faces_hbm,
    out_ref,
    colors,
    rhs,
    old,
    inv,
    faces,
    halo_left,
    halo_right,
    below,
    sent,
    got,
    matrices,
    offsets,
    parts,
    weights,
    turned,
    arrived,
    leaving,
    load_sem,
    send_sem,
    recv_sem,
    order_sem,
    ready_right,
    ready_later,
):
    flow, cross = lax.axis_index("flow"), lax.axis_index("cross")
    core = lax.rem(flow, 2)
    odd = core == 1
    has_left, has_right = cross > 0, cross < crosses - 1
    has_upper, has_lower = flow > 0, flow < flows - 1
    inner = flow > 1

    def among(*layers):
        return functools.reduce(jnp.logical_or, [flow == layer for layer in layers])

    before, express = among(19, 26, 27, 30, 31), among(9, 13, 21)
    more = jnp.where(
        flow == 9, 1, jnp.where(flow == 13, 3, jnp.where(among(19, 21, 26, 27, 30, 31), 2, 0))
    )
    passes = among(27, 31)
    helper = among(10, 11, 14, 15, 16, 17, 22, 23, 24, 25, 28, 29)
    signals, goes_after = among(22, 25, 29), among(23, 24, 28)
    to_site_step = jnp.where(
        among(10, 14, 22),
        -1,
        jnp.where(among(15, 23), -2, jnp.where(odd, 2, 3)),
    )
    relayed, relays = among(15, 16), among(4, 10)
    to_site_box = jnp.where(flow == 15, 3, 1 + core)

    def at(flow_step, cross_step):
        return (flow + flow_step, cross + cross_step)

    barrier = pltpu.get_barrier_semaphore()
    earlier_ones = [(has_upper, at(-1, 0)), (odd & (flow >= 2), at(-2, 0))]
    later_ones = [(has_lower, at(1, 0)), (odd & (flow < flows - 2), at(2, 0))]
    for distance, layers in (
        (3, (13, 16, 21, 24, 27, 28)),
        (4, (9, 13, 21, 27)),
        (5, (21,)),
        (6, (10, 13, 21)),
        (9, (4, 10)),
        (11, (4,)),
    ):
        later_ones.append((among(*layers), at(distance, 0)))
        earlier_ones.append((among(*(layer + distance for layer in layers)), at(-distance, 0)))

    def block_load(place, face, j, k):
        source = inv_hbm.at[0] if face is None else faces_hbm.at[0, face]
        target = inv if face is None else faces.at[face]
        return pltpu.make_async_copy(
            source.at[j, :, k, :], target.at[j, k], load_sem.at[place]
        )

    cells = [(j, k) for j in (0, 1) for k in (0, 1)]
    span_blocks = [(4, 0, 1), (4, 1, 1), (5, 0, 0), (5, 1, 0)]
    groups = [
        [(None, *cell) for cell in cells],
        [(0, *cell) for cell in cells],
        span_blocks + [(face, *cell) for face in (2, 3) for cell in cells],
        [(1, *cell) for cell in cells],
    ]
    count, loads = 0, []
    for group in groups:
        loads.append([block_load(count + n, *block) for n, block in enumerate(group)])
        count += len(group)
    old_load = pltpu.make_async_copy(old_hbm.at[0], old, load_sem.at[count])
    rhs_load = pltpu.make_async_copy(rhs_hbm.at[0], rhs, load_sem.at[count + 1])
    color_load = pltpu.make_async_copy(color_hbm.at[0], colors, load_sem.at[count + 2])
    color_load.start()
    old_load.start()
    rhs_load.start()

    @pl.when(inner)
    def _():
        for n in (0, 1, 2, 3):
            for load in loads[n]:
                load.start()

    @pl.when(~inner)
    def _():
        for n in (2, 3, 0, 1):
            for load in loads[n]:
                load.start()

    def counted(devices):
        return sum(present.astype(jnp.int32) for present, _ in devices)

    def tell(semaphore, devices):
        for present, device in devices:

            @pl.when(present)
            def _(device=device):
                pl.semaphore_signal(
                    semaphore, inc=1, device_id=device, device_id_type=MESH
                )

    tell(barrier, [(has_right, at(0, 1))] + later_ones)

    offsets[OWN] = jnp.zeros((8, WIDE), F32)
    @pl.when(has_left | has_upper)
    def _():
        pl.semaphore_wait(barrier, has_left.astype(jnp.int32) + counted(earlier_ones))

    tell(ready_right, [(has_left, at(0, -1))])

    def remote(source, target, places, device):
        sending, receiving = places if isinstance(places, tuple) else (places, places)
        return pltpu.make_async_remote_copy(
            src_ref=source,
            dst_ref=target,
            send_sem=send_sem.at[sending],
            recv_sem=recv_sem.at[receiving],
            device_id=device,
            device_id_type=MESH,
        )

    halos = [
        (has_right, has_left, remote(old_hbm.at[0, 1], halo_left, 0, at(0, 1))),
        (has_left, has_right, remote(old_hbm.at[0, 0], halo_right, 1, at(0, -1))),
        (has_upper, has_lower, remote(old_hbm.at[0], below, 2, at(-1, 0))),
    ]
    for sends, _, halo in halos[1:]:
        pl.when(sends)(halo.start)
    tell(ready_later, earlier_ones)

    @pl.when(has_right)
    def _():
        pl.semaphore_wait(ready_right, 1)
        halos[0][2].start()

    color_load.wait()
    even = colors[0, 0] == 0

    def pick(first, second):
        return jnp.where(even, first, second)

    def cross_face(e):
        return faces[3 - e // 2, e // 2, e % 2]

    def span_face(e):
        return faces[5 - e % 2, e // 2, e % 2]

    def out_face(e):
        return faces[2 + e // 2, e // 2, e % 2]

    def inverse(e):
        return inv[e // 2, e % 2]

    def in_parts(source, target, sending, receiving, flow_step):
        return [
            remote(
                source.at[pl.ds(PART * n, PART)],
                target.at[pl.ds(PART * n, PART)],
                (sending + n, receiving + n),
                at(flow_step, 0),
            )
            for n in range(PARTS)
        ]

    def received(box):
        return 3 + PARTS * box

    to_second = in_parts(sent, got.at[0], 3, received(0), 1)
    to_site = in_parts(
        sent,
        got.at[jnp.where(relayed, 1, to_site_box)],
        7,
        jnp.where(relayed, 29, received(to_site_box)),
        jnp.where(flow == 15, -11, jnp.where(flow == 16, -6, to_site_step)),
    )
    relay_box = jnp.where(flow == 4, 3, 1)
    to_relay = in_parts(sent, got.at[1], 32, 29, -1)
    relay = in_parts(got.at[1], got.at[relay_box], 32, received(relay_box), 9)

    @pl.when(~inner)
    def _():
        for load in loads[2]:
            load.wait()

    @pl.when(inner)
    def _():
        sent[...] = jnp.zeros_like(sent)
        for slot in (OWN, FIRST, FAR, FAR + 1, FAR + 2):
            matrices[slot, ROWS:] = jnp.zeros((WIDE - ROWS, WIDE), F32)
        for slot in (CHIP, MORE + 1, MORE + 2, MORE + 3):
            matrices[slot, TWICE:] = jnp.zeros((WIDE - TWICE, WIDE), F32)
        for n in (0, 1):
            for load in loads[n]:
                load.wait()
        diagonal = [-product(inverse(e), faces[0, e // 2, e % 2]) for e in range(4)]
        from_a, from_d = pick(diagonal[0], diagonal[1]), pick(diagonal[3], diagonal[2])
        put_block(sent, 0, from_a)
        put_block(sent, 1, from_d)
        put_block(sent, 2, pick(diagonal[1], diagonal[0]))
        put_block(sent, 3, pick(diagonal[2], diagonal[3]))
        for e in range(4):
            put_side(sent, e, e, diagonal[e])
        for load in loads[2]:
            load.wait()
        inv_b, inv_c = pick(inverse(1), inverse(0)), pick(inverse(2), inverse(3))
        gain_ba = product(inv_b, pick(span_face(1), span_face(0)))
        gain_bd = product(inv_b, pick(cross_face(1), cross_face(0)))
        gain_ca = product(inv_c, pick(cross_face(2), cross_face(3)))
        gain_cd = product(inv_c, pick(span_face(2), span_face(3)))
        for slot, source, gain, here, there in (
            (4, from_a, gain_ba, (1, 0), (0, 1)),
            (5, from_d, gain_bd, (1, 3), (0, 2)),
            (6, from_a, gain_ca, (2, 0), (3, 1)),
            (7, from_d, gain_cd, (2, 3), (3, 2)),
        ):
            block = -product(gain, source)
            nothing = jnp.zeros_like(block)
            put_block(sent, slot, block)
            put_side(sent, *here, pick(block, nothing))
            put_side(sent, *there, pick(nothing, block))
        sent[FLAG:] = jnp.where(even, 1.0, 0.0) + jnp.zeros((SENT - FLAG, 128), F32)
        @pl.when(has_lower)
        def _():
            pl.semaphore_wait(ready_later, counted(later_ones))

        for copy in to_site:
            pl.when(helper & ~goes_after)(copy.start)
        for copy in to_second:
            pl.when(~odd)(copy.start)
        spread(matrices.at[OWN], sent)
        matrices[OWN, ROWS:TWICE] = matrices[OWN, MAIN:ROWS]

    old_load.wait()
    rhs_load.wait()
    held = [old[e // 2, e % 2] for e in range(4)]
    old_b, old_c = pick(held[1], held[0]), pick(held[2], held[3])
    around_a = times_block(old_c, pick(cross_face(0), cross_face(1))) + times_block(
        old_b, pick(span_face(0), span_face(1))
    )
    around_d = times_block(old_b, pick(cross_face(3), cross_face(2))) + times_block(
        old_c, pick(span_face(3), span_face(2))
    )

    for load in loads[3]:
        load.wait()

    for _, receives, halo in halos:
        pl.when(receives)(halo.wait_recv)

    def part(e):
        j, k = e // 2, e % 2
        halo = jnp.where(*((has_left, halo_left[k]) if j == 0 else (has_right, halo_right[k])), 0.0)
        under = jnp.where(has_lower, below[j, k], 0.0)
        return (
            rhs[j, k]
            - times_block(under, faces[1, j, k])
            - times_block(halo, out_face(e))
        )

    for e in range(4):
        parts[e] = part(e)

    own_offset, first_offset = offsets.at[OWN], offsets.at[FIRST]
    offset_to_second = remote(own_offset, first_offset, (11, 23), at(1, 0))
    offset_to_site = remote(
        own_offset, offsets.at[2 + to_site_box], (12, 23 + to_site_box), at(to_site_step, 0)
    )

    @pl.when(flow == 1)
    def _():
        for load in loads[1]:
            load.wait()
        offset_to_second.wait_recv()
        for e in range(4):
            upper = jnp.concatenate(
                [
                    first_offset[:, 128 * e : 128 * e + 128],
                    first_offset[:, MAIN + 8 * e : MAIN + 8 * e + 7],
                ],
                axis=1,
            )
            parts[e] = parts[e] - times_block(upper, faces[0, e // 2, e % 2])

    total_a = pick(parts[0], parts[1]) - around_a
    total_d = pick(parts[3], parts[2]) - around_d

    @pl.when(~inner)
    def _():
        for load in loads[0]:
            load.wait()

    new_a = times_block(total_a, pick(inverse(0), inverse(1)))
    new_d = times_block(total_d, pick(inverse(3), inverse(2)))
    total_b = pick(parts[1], parts[0]) - (
        times_block(new_d, pick(cross_face(1), cross_face(0)))
        + times_block(new_a, pick(span_face(1), span_face(0)))
    )
    total_c = pick(parts[2], parts[3]) - (
        times_block(new_a, pick(cross_face(2), cross_face(3)))
        + times_block(new_d, pick(span_face(2), span_face(3)))
    )
    new_b = times_block(total_b, pick(inverse(1), inverse(0)))
    new_c = times_block(total_c, pick(inverse(2), inverse(3)))
    put_rows(own_offset, 0, pick(new_a, new_b))
    put_rows(own_offset, 1, pick(new_b, new_a))
    put_rows(own_offset, 2, pick(new_c, new_d))
    put_rows(own_offset, 3, pick(new_d, new_c))

    @pl.when(~inner)
    def _():
        pl.semaphore_wait(ready_later, counted(later_ones))

    pl.when(~odd)(offset_to_second.start)
    pl.when(helper)(offset_to_site.start)

    @pl.when(signals)
    def _():
        for copy in to_site[:2]:
            copy.wait_send()
        pl.semaphore_signal(
            order_sem, inc=1, device_id=at(1 - 2 * core, 0), device_id_type=MESH
        )

    @pl.when(goes_after)
    def _():
        pl.semaphore_wait(order_sem, 1)
        for copy in to_site:
            copy.start()

    @pl.when(relays)
    def _():
        for arriving, onward in zip(to_relay, relay):
            arriving.wait_recv()
            onward.start()

    def state(slot, send_place, flow_step):
        return remote(leaving.at[slot], arrived, (send_place, 28), at(flow_step, 0))

    sends = [
        (flow == 27, state(1, 13, 4)),
        (flow == 27, state(1, 14, 3)),
        (odd & ~among(11, 15, 17, 23, 25, 29, 31), state(1, 15, 2)),
        (odd & ~among(15, 23, 25, 29, 31), state(1, 16, 1)),
    ]
    express_sends = [
        (among(13, 21), state(0, 17, 6)),
        (flow == 21, state(0, 18, 5)),
        (express, state(0, 19, 4)),
        (among(13, 21), state(0, 20, 3)),
    ]
    receives_state = sends[0][1].wait_recv

    def passed(box):
        first = 17 + 5 * box
        offset = offsets.at[2 + box]
        return in_parts(got.at[box], got.at[box], first, received(box), -1) + [
            remote(offset, offset, (first + PARTS, 23 + box), at(-1, 0))
        ]

    @pl.when(~inner)
    def _():
        leaving[1] = own_offset[...]
        for present, copy in sends:
            pl.when(present)(copy.start)

    @pl.when(inner)
    def _():
        base = jnp.where(odd, CHIP, OWN)
        own_used = jnp.where(flow == 13, MORE + 1, CHIP)

        def compose(turn, carry):
            box = jnp.where((turn == 0) | (turn == 3) | among(9, 21), turn, 3 - turn)
            layer = jnp.where(turn == 0, FIRST, 2 + box)
            held = jnp.where(turn == 0, OWN, jnp.where(turn == 1, base, MORE - 1 + turn))
            result = jnp.where(turn == 0, CHIP, MORE + turn)
            held_later = (turn == 0) | before | ((flow == 13) & (turn == 1))
            later = jnp.where(held_later, held, layer)
            earlier = jnp.where(held_later, layer, held)
            for copy in in_parts(sent, got.at[box], 3, received(box), -1):
                copy.wait_recv()
            remote(own_offset, offsets.at[layer], (11, 23 + box), at(-1, 0)).wait_recv()

            @pl.when(passes & (turn > 0))
            def _():
                for copy in passed(box):
                    copy.start()

            spread(matrices.at[layer], got.at[box])
            matrices[result, :TWICE] = composed(weights, matrices[later], matrices[earlier])
            offsets[result] = step(offsets[earlier], weights[...]) + offsets[later]
            return carry

        lax.fori_loop(1 - core, 1 + more, compose, 0)

        used = jnp.where(more > 0, MORE + more, base)
        pack_turned(turned.at[0], matrices[used])

        turns = jnp.where(express, 3, 2)

        def advance(turn, carry):
            pl.when(turn == 1)(receives_state)
            last = turn == turns - 1
            own = express & last

            @pl.when(own)
            def _():
                pack_turned(turned.at[1], matrices[own_used])

            rows = arrived[...]
            moved = fast_step(rows, turned.at[jnp.where(own, 1, 0)])
            leaving[jnp.where(last, 1, 0)] = moved + offsets[jnp.where(own, own_used, used)]

            @pl.when(express & (turn == 1))
            def _():
                for present, copy in express_sends:
                    pl.when(present)(copy.start)

            @pl.when(last)
            def _():
                for present, copy in sends:
                    pl.when(present)(copy.start)

            return carry

        lax.fori_loop(1, turns, advance, 0)

    rows = leaving[1]
    for e in range(4):
        out_ref[0, e // 2, e % 2, :, :128] = rows[:, 128 * e : 128 * e + 128]
        out_ref[0, e // 2, e % 2, :, 128:] = rows[:, MAIN + 8 * e : MAIN + 8 * e + 7]

    for present, copy in sends:
        pl.when(present)(copy.wait_send)

    for present, copy in express_sends:
        pl.when(present)(copy.wait_send)

    @pl.when(passes)
    def _():
        for box in (1, 2):
            for copy in passed(box):
                copy.wait_send()

    @pl.when(flow == 0)
    def _():
        for load in loads[1]:
            load.wait()

    for copy in to_second:
        pl.when(inner & ~odd)(copy.wait_send)
    pl.when(~odd)(offset_to_second.wait_send)
    for n, copy in enumerate(to_site):
        pl.when(helper & ~signals if n < 2 else helper)(copy.wait_send)
    for copy in relay:
        pl.when(relays)(copy.wait_send)
    pl.when(helper)(offset_to_site.wait_send)
    for sends, _, halo in halos:
        pl.when(sends)(halo.wait_send)


def body(flows, crosses, right_side, start_iterate, inverse_blocks, face_blocks, color_order):
    _, columns, spans, vectors, width = right_side.shape
    hbm = pl.BlockSpec(memory_space=pltpu.HBM)
    return pl.pallas_call(
        functools.partial(kernel, flows, crosses),
        out_shape=jax.ShapeDtypeStruct(right_side.shape, F32),
        in_specs=[hbm] * 5,
        out_specs=pl.BlockSpec(memory_space=pltpu.VMEM),
        scratch_shapes=[
            pltpu.SMEM((columns, spans), jnp.int32),
            pltpu.VMEM((columns, spans, vectors, width), F32),
            pltpu.VMEM((columns, spans, vectors, width), F32),
            pltpu.VMEM((columns, spans, width, width), F32),
            pltpu.VMEM((6, columns, spans, width, width), F32),
            pltpu.VMEM((spans, vectors, width), F32),
            pltpu.VMEM((spans, vectors, width), F32),
            pltpu.VMEM((columns, spans, vectors, width), F32),
            pltpu.VMEM((SENT, 128), F32),
            pltpu.VMEM((4, SENT, 128), F32),
            pltpu.VMEM((9, WIDE, WIDE), F32),
            pltpu.VMEM((9, vectors, WIDE), F32),
            pltpu.VMEM((2 * columns, vectors, width), F32),
            pltpu.VMEM((WIDE, DEEP), BF16),
            pltpu.VMEM((2, DEEP, WIDE), BF16),
            pltpu.VMEM((vectors, WIDE), F32),
            pltpu.VMEM((2, vectors, WIDE), F32),
            pltpu.SemaphoreType.DMA((27,)),
            pltpu.SemaphoreType.DMA((36,)),
            pltpu.SemaphoreType.DMA((33,)),
            pltpu.SemaphoreType.REGULAR,
            pltpu.SemaphoreType.REGULAR,
            pltpu.SemaphoreType.REGULAR,
        ],
        compiler_params=pltpu.CompilerParams(
            collective_id=0, has_side_effects=True, vmem_limit_bytes=(54 * 1024 - 128) * 1024
        ),
        cost_estimate=pl.CostEstimate(flops=10**9, bytes_accessed=4 * 10**6, transcendentals=0),
        name="sweep_chain",
    )(
        color_order,
        right_side,
        start_iterate,
        inverse_blocks.transpose(0, 1, 3, 2, 4),
        face_blocks.transpose(0, 1, 2, 4, 3, 5),
    )


def solution(mesh):
    return jax.shard_map(
        functools.partial(body, mesh.shape["flow"], mesh.shape["cross"]),
        mesh=mesh,
        in_specs=(
            P("flow", "cross", None, None, None),
            P("flow", "cross", None, None, None),
            P("flow", "cross", None, None, None),
            P("flow", None, "cross", None, None, None),
            P("flow", "cross", None),
        ),
        out_specs=P("flow", "cross", None, None, None),
        check_vma=False,
    )
```
